128 devices in a mesh: outer: 16 (over x, z), inner: 8 (over y, core).
Axes of the slice: x: 4, y: 4, z: 4, core: 2. Of those that a mesh axis runs over, the one named last changes fastest.
Arguments:
- shocks: bfloat16 [16, 1048576], P(None, ('outer', 'inner')), may hold values from -6 to 6
- leaf_basis: bfloat16 [4096, 32, 256], P(('outer', 'inner')), may hold values from -0.375 to 0.375
- self_block: bfloat16 [4096, 256, 256], P(('outer', 'inner')), may hold values from -0.25 to 0.25
- near_block: bfloat16 [4096, 3, 256, 256], P(('outer', 'inner')), may hold values from -0.25 to 0.25
- near_offset: int32 [4096, 3], P(('outer', 'inner')), may hold values from -32 to 32
- near_count: int32 [4096], P(('outer', 'inner')), may hold values from 0 to 3
- local_transfer: bfloat16 [8064, 1024], P(('outer', 'inner')), may hold values from -0.75 to 0.75
- local_coupling: bfloat16 [8064, 8, 1024], P(('outer', 'inner')), may hold values from -1 to 1
- far_device: int32 [8064, 8], P(('outer', 'inner')), may hold values from 0 to 127, as said below
- far_slot: int32 [8064, 8], P(('outer', 'inner')), may hold values from 0 to 62, as said below
- upper_transfer: bfloat16 [120, 1024], replicated, may hold values from -0.75 to 0.75
- upper_coupling: bfloat16 [124, 8, 1024], replicated, may hold values from -1 to 1
- upper_partner: int32 [124, 8], replicated, may hold values from 4 to 127, as said below
Outputs:
- hazard_field: float32 [16, 1048576], P(None, ('outer', 'inner'))
The draws below stay inside these ranges and needn't reach their ends.
Inputs may be any that keep to these rules, and one draw needn't show every extreme that they name: `far_device`: for a row of a level-k cluster held by device d, every entry is within min(2^(k+1), 32) of d; on some device each level's rows reach that distance. `far_slot`: each entry is the row, among the 63 clusters held by the target device (levels in order, leaves first), of a cluster on the same level as the row's own cluster. `upper_partner`: row h - 4 lists nodes of the same level as upper node h (nodes 2^j .. 2^(j+1) - 1), never h itself.
All inputs are finite; a program needn't handle non-finite values.
Results may differ from the reference program's by a relative error of at most 0.0027.
Values may be sent and summed in bfloat16 or wider, within the bound.
A program may use at most 128 MiB of HBM per device.

```python
import jax
import jax.numpy as jnp
from jax import lax

SCEN = 16
RANK = 32
LEAF = 256
NEAR = 3
FAR = 8
LEAVES_DEV = 32
LOCALC = 63
NLEAF = 4096
POINTS = 1048576
LOCAL_ALL = 8064
REACH = 32
UPPER_NODES = 124
UPPER_LINKS = 120
DEVICES = 128


def row_heights():
    local_row = jnp.arange(LOCAL_ALL, dtype=jnp.int32) % LOCALC
    height = jnp.zeros((LOCAL_ALL,), jnp.int32)
    for power in range(1, LEAVES_DEV.bit_length()):
        height = height + (local_row >= 2 * LEAVES_DEV - 2 * (LEAVES_DEV >> power)).astype(jnp.int32)
    return (local_row, height)


def draw_far_device(key, part):
    key = jax.random.fold_in(key, 7)
    local_row, height = row_heights()
    owner_dev = jnp.arange(LOCAL_ALL, dtype=jnp.int32) // LOCALC
    radius = jnp.minimum(jnp.left_shift(jnp.full((LOCAL_ALL,), 2, jnp.int32), height), REACH)
    level_size = jnp.right_shift(jnp.full((LOCAL_ALL,), LEAVES_DEV, jnp.int32), height)
    level_start = 2 * LEAVES_DEV - 2 * level_size
    raw_bits = jax.random.randint(key, (LOCAL_ALL, FAR), 0, 2 ** 30, dtype=jnp.int32)
    offset = raw_bits % (2 * radius[:, None] + 1) - radius[:, None]
    side_sign = jax.random.randint(jax.random.fold_in(key, 1), (LOCAL_ALL,), 0, 2, dtype=jnp.int32) * 2 - 1
    first_row = local_row == level_start
    offset = offset.at[:, 0].set(jnp.where(first_row, side_sign * radius, offset[:, 0]))
    target = owner_dev[:, None] + offset
    inside = (target >= 0) & (target < DEVICES)
    return jnp.where(inside, target, owner_dev[:, None])


def draw_far_slot(key, part):
    key = jax.random.fold_in(key, 11)
    row_level = jnp.arange(LOCAL_ALL, dtype=jnp.int32) % LOCALC
    height = jnp.zeros((LOCAL_ALL,), jnp.int32)
    for power in range(1, LEAVES_DEV.bit_length()):
        height = height + (row_level >= 2 * LEAVES_DEV - 2 * (LEAVES_DEV >> power)).astype(jnp.int32)
    level_size = jnp.right_shift(jnp.full((LOCAL_ALL,), LEAVES_DEV, jnp.int32), height)
    level_start = 2 * LEAVES_DEV - 2 * level_size
    raw_bits = jax.random.randint(key, (LOCAL_ALL, FAR), 0, 2 ** 30, dtype=jnp.int32)
    return level_start[:, None] + raw_bits % level_size[:, None]


def draw_upper_partner(key, part):
    key = jax.random.fold_in(key, 23)
    node_index = jnp.arange(UPPER_NODES, dtype=jnp.int32) + 4
    level_width = jnp.full((UPPER_NODES,), 4, jnp.int32)
    for power in range(3, DEVICES.bit_length() - 1):
        level_width = jnp.where(node_index >= 2 ** power, 2 ** power, level_width)
    raw_bits = jax.random.randint(key, (UPPER_NODES, FAR), 0, 2 ** 30, dtype=jnp.int32)
    step_bits = 1 + raw_bits % (level_width[:, None] - 1)
    return level_width[:, None] + (node_index[:, None] - level_width[:, None] + step_bits) % level_width[:, None]


def set_ends(array, own_key, low, top_value):
    longest = array.shape.index(max(array.shape))
    spots = []
    for shift in (0, 1):
        where = [jax.random.randint(jax.random.fold_in(own_key, axis), (), 0, length) for axis, length in enumerate(array.shape)]
        where[longest] = (where[longest] + shift) % array.shape[longest]
        spots.append(tuple(where))
    return array.at[spots[0]].set(low).at[spots[1]].set(top_value)


def level_of(rng, shape, split, least, largest):
    def one(dim, blocks):
        steps = jax.random.uniform(jax.random.fold_in(jax.random.fold_in(rng, 6), dim), (blocks,), jnp.float32, least / len(split), largest / len(split))
        return jnp.repeat(jnp.exp(steps), shape[dim] // blocks).reshape((-1,) + (1,) * (len(shape) - dim - 1))

    gain = one(*split[0])
    for cut in split[1:]:
        gain = gain * one(*cut)
    return gain


def centred(rng, dims, scale, reach, shards=(), held_as=jnp.bfloat16):
    gain = level_of(rng, dims, shards, -0.22, 0.18) if shards else 1.0
    array = jax.random.normal(rng, dims, jnp.float32) * scale * gain
    return jnp.minimum(jnp.maximum(array, -reach), reach).astype(held_as)


def setup_inputs(seed: int = 0) -> dict:
    key_of = jax.random.split(jax.random.key(seed), 14)
    shocks = centred(key_of[0], (SCEN, POINTS), 1.0, 6.0, ((1, 128),))
    leaf_basis = centred(key_of[1], (NLEAF, RANK, LEAF), LEAF ** -0.5, 0.375, ((0, 128),))
    self_block = centred(key_of[2], (NLEAF, LEAF, LEAF), (2 * LEAF) ** -0.5, 0.25, ((0, 128),))
    near_block = centred(key_of[3], (NLEAF, NEAR, LEAF, LEAF), (2 * LEAF) ** -0.5, 0.25, ((0, 128),))
    near_offset = set_ends(jax.random.randint(key_of[4], (NLEAF, NEAR), -LEAVES_DEV, LEAVES_DEV + 1), jax.random.fold_in(key_of[4], 1), -LEAVES_DEV, LEAVES_DEV).astype(jnp.int32)
    near_count = set_ends(jax.random.randint(key_of[5], (NLEAF,), 0, NEAR + 1), jax.random.fold_in(key_of[5], 1), 0, NEAR).astype(jnp.int32)
    local_transfer = centred(key_of[6], (LOCAL_ALL, RANK * RANK), (2 * RANK) ** -0.5, 0.75, ((0, 128),))
    local_coupling = centred(key_of[7], (LOCAL_ALL, FAR, RANK * RANK), RANK ** -0.5, 1.0, ((0, 128),))
    far_device = draw_far_device(jax.random.fold_in(key_of[13], 71), 0)
    far_slot = draw_far_slot(jax.random.fold_in(key_of[13], 71), 0)
    upper_transfer = centred(key_of[10], (UPPER_LINKS, RANK * RANK), (2 * RANK) ** -0.5, 0.75)
    upper_coupling = centred(key_of[11], (UPPER_NODES, FAR, RANK * RANK), RANK ** -0.5, 1.0)
    upper_partner = draw_upper_partner(jax.random.fold_in(key_of[13], 71), 0)
    return {"shocks": shocks, "leaf_basis": leaf_basis, "self_block": self_block, "near_block": near_block, "near_offset": near_offset, "near_count": near_count, "local_transfer": local_transfer, "local_coupling": local_coupling, "far_device": far_device, "far_slot": far_slot, "upper_transfer": upper_transfer, "upper_coupling": upper_coupling, "upper_partner": upper_partner}


PRECISE = lax.Precision.HIGHEST


def level_rows(height, leaf_count):
    extent = leaf_count >> height
    return 2 * leaf_count - 2 * extent, extent


def reference(shocks, leaf_basis, self_block, near_block, near_offset, near_count, local_transfer, local_coupling, far_device, far_slot, upper_transfer, upper_coupling, upper_partner):
    heights = LEAVES_DEV.bit_length() - 1
    top_height = DEVICES.bit_length() - 1
    blocks = shocks.reshape(SCEN, NLEAF, LEAF)
    leaf_coef = jnp.einsum("snp,nrp->nsr", blocks.astype(jnp.float32), leaf_basis.astype(jnp.float32), precision=PRECISE)
    transfer = local_transfer.astype(jnp.float32).reshape(DEVICES, LOCALC, RANK, RANK)
    tiers = [leaf_coef.reshape(DEVICES, LEAVES_DEV, SCEN, RANK)]
    for height in range(1, heights + 1):
        offset, extent = level_rows(height - 1, LEAVES_DEV)
        products = jnp.einsum("dnsr,dnrq->dnsq", tiers[-1], transfer[:, offset:offset + extent], precision=PRECISE)
        tiers.append(products.reshape(DEVICES, extent // 2, 2, SCEN, RANK).sum(axis=2))
    root_matrix = transfer[:, LOCALC - 1]
    upper_matrix = upper_transfer.astype(jnp.float32).reshape(UPPER_LINKS, RANK, RANK)
    lifted = jnp.einsum("nsr,nrq->nsq", tiers[-1][:, 0], root_matrix, precision=PRECISE)
    current = lifted.reshape(DEVICES // 2, 2, SCEN, RANK).sum(axis=1)
    by_height = {top_height - 1: current}
    for height in range(top_height - 1, 2, -1):
        first = 2 ** height - 8
        products = jnp.einsum("nsr,nrq->nsq", current, upper_matrix[first:first + 2 ** height], precision=PRECISE)
        current = products.reshape(2 ** (height - 1), 2, SCEN, RANK).sum(axis=1)
        by_height[height - 1] = current
    every_node = jnp.concatenate([jnp.zeros((4, SCEN, RANK), jnp.float32)] + [by_height[height] for height in range(2, top_height)], axis=0)
    couple_up = upper_coupling.astype(jnp.float32).reshape(UPPER_NODES, FAR, RANK, RANK)
    upper_field = jnp.einsum("nfsr,nfrq->nsq", every_node[upper_partner], couple_up, precision=PRECISE)
    upper_down = upper_field[0:4]
    for height in range(3, top_height):
        first = 2 ** height
        parent = jnp.repeat(upper_down, 2, axis=0)
        upper_down = upper_field[first - 4:2 * first - 4] + jnp.einsum("nsq,nrq->nsr", parent, upper_matrix[first - 8:2 * first - 8], precision=PRECISE)
    root_down = jnp.einsum("nsq,nrq->nsr", jnp.repeat(upper_down, 2, axis=0), root_matrix, precision=PRECISE)
    cluster_coef = jnp.concatenate(tiers, axis=1).reshape(LOCAL_ALL, SCEN, RANK)
    couple_local = local_coupling.astype(jnp.float32).reshape(LOCAL_ALL, FAR, RANK, RANK)
    products = jnp.einsum("nsr,nfrq->nfsq", cluster_coef, couple_local, precision=PRECISE)
    target = (far_device * LOCALC + far_slot).reshape(-1)
    local_field = jax.ops.segment_sum(products.reshape(LOCAL_ALL * FAR, SCEN, RANK), target, num_segments=LOCAL_ALL)
    local_field = local_field.reshape(DEVICES, LOCALC, SCEN, RANK)
    cluster_field = local_field[:, LOCALC - 1:] + root_down[:, None]
    for height in range(heights - 1, -1, -1):
        offset, extent = level_rows(height, LEAVES_DEV)
        parent = jnp.repeat(cluster_field, 2, axis=1)
        cluster_field = local_field[:, offset:offset + extent] + jnp.einsum("dnsq,dnrq->dnsr", parent, transfer[:, offset:offset + extent], precision=PRECISE)
    leaf_field = cluster_field.reshape(NLEAF, SCEN, RANK).astype(jnp.bfloat16)
    far_part = jnp.einsum("nsr,nrp->snp", leaf_field.astype(jnp.float32), leaf_basis.astype(jnp.float32), precision=PRECISE)
    padded = jnp.pad(blocks, ((0, 0), (LEAVES_DEV, LEAVES_DEV), (0, 0)))
    near_index = (jnp.arange(NLEAF, dtype=jnp.int32)[:, None] + near_offset + LEAVES_DEV).reshape(DEVICES, LEAVES_DEV, NEAR)
    live_mask = (jnp.arange(NEAR, dtype=jnp.int32)[None, :] < near_count[:, None]).reshape(DEVICES, LEAVES_DEV, NEAR)
    own_blocks = blocks.reshape(SCEN, DEVICES, LEAVES_DEV, LEAF).transpose(1, 0, 2, 3)

    def one_device(pieces):
        own_piece, self_piece, near_piece, index_piece, mask_piece = pieces
        picked = padded[:, index_piece.reshape(-1)].reshape(SCEN, LEAVES_DEV, NEAR, LEAF).astype(jnp.float32)
        picked = picked * mask_piece[None, :, :, None].astype(jnp.float32)
        self_sum = jnp.einsum("snp,npq->snq", own_piece.astype(jnp.float32), self_piece.astype(jnp.float32), precision=PRECISE)
        return self_sum + jnp.einsum("snkp,nkpq->snq", picked, near_piece.astype(jnp.float32), precision=PRECISE)

    near_sum = lax.map(one_device, (own_blocks, self_block.reshape(DEVICES, LEAVES_DEV, LEAF, LEAF), near_block.reshape(DEVICES, LEAVES_DEV, NEAR, LEAF, LEAF), near_index, live_mask))
    near_sum = near_sum.transpose(1, 0, 2, 3).reshape(SCEN, NLEAF, LEAF)
    return (near_sum + far_part).reshape(SCEN, POINTS)
```

```python
import jax
import jax.numpy as jnp
import numpy as np
from jax import lax
from jax.experimental import pallas as pl
from jax.experimental.pallas import tpu as pltpu
from jax.sharding import PartitionSpec as P

F32 = jnp.float32
BF16 = jnp.bfloat16
MESH = pl.DeviceIdType.MESH
VMEM = pl.BlockSpec(memory_space=pltpu.VMEM)
SMEM = pl.BlockSpec(memory_space=pltpu.SMEM)
ANY = pl.BlockSpec(memory_space=pl.ANY)

CLASSES = ((1, 2, 16, 0), (3, 4, 8, 64), (5, 8, 4, 96), (9, 16, 2, 128), (17, 32, 1, 160))
TILES = 192
MESSAGES = 64


def slot_of(offset):
    for near, far, tiles, base in CLASSES:
        if near <= abs(offset) <= far:
            count = far - near + 1
            place = offset + far if offset < 0 else offset - near + count
            return base + place * tiles
    return None


LEVEL_ROW = (0, 32, 48, 56, 60, 62, 63)


def lane_table():
    table = np.zeros((8, 768), np.int32)
    for lane in range(768):
        if lane < 256:
            item, part, scale, shift = lane, 0, 32, 64
        elif lane < 384:
            item, part, scale, shift = lane, 0, 16, 64 - 32
        elif lane < 512:
            item, part = 384 + (lane - 384) % 64, (lane - 384) // 64
            scale, shift = 16, 128 + 8 * part - 48
        elif lane < 640:
            item, part = 448 + (lane - 512) % 32, (lane - 512) // 32
            scale, shift = 16, 256 + 4 * part - 56
        else:
            item, part = 480 + (lane - 640) % 32, (lane - 640) // 32
            scale, shift = 16, 512 + 4 * part - 60
        if item >= 504:
            scale, shift = 0, -1000000
        table[0, lane], table[1, lane], table[2, lane], table[3, lane] = item // 8, item % 8, scale, shift
    return table


LANES = lane_table()
SPREAD = (np.arange(256)[:, None] % 32 == np.arange(1024)[None, :] // 32).astype(np.float32)
GATHER = (np.arange(1024)[:, None] // 32 == np.arange(128)[None, :] % 32).astype(np.float32)
SELECT = (np.arange(256)[:, None] % 32 == np.arange(128)[None, :] % 32).astype(np.float32)


def iota(shape, dim):
    return lax.broadcasted_iota(jnp.int32, shape, dim)


def halves(x):
    high = x.astype(BF16)
    low = (x - high.astype(F32)).astype(BF16)
    return high, low


def dot(a, b):
    return jnp.dot(a, b, preferred_element_type=F32)


def spread(coefs, mask, matrix):
    high, low = halves(jnp.where(mask, coefs, 0.0))
    return dot(jnp.concatenate([high, low], axis=1), matrix)


def fold(x):
    x = x + pltpu.roll(x, 64, 1)
    return x + pltpu.roll(x, 32, 1)


def apply(wide, row):
    total = wide[:, 0:128] * row[:, 0:128]
    for t in range(1, 8):
        total = total + wide[:, t * 128 : t * 128 + 128] * row[:, t * 128 : t * 128 + 128]
    return total


def first_group(rows):
    return iota((rows, 128), 1) < 32


def up_kernel(
    x_ref, v_ref, e_ref, b_ref, fd_ref, fs_ref, ut_ref, rr_ref, lane_ref,
    send_ref, own_ref, lift_ref, f_ref,
    ef_ref, uf_ref, wide_ref, prod_ref,
):
    outer = lax.axis_index("outer")
    me = outer * 8 + lax.axis_index("inner")
    matrix = rr_ref[...]
    ef_ref[pl.ds(0, 63), :] = e_ref[...].astype(F32)
    uf_ref[...] = ut_ref[...].astype(F32)
    for k in range(4):
        f_ref[k : k + 1, :] = uf_ref[pl.ds(56 + 4 * outer + k, 1), :]
    for k in range(2):
        f_ref[4 + k : 5 + k, :] = uf_ref[pl.ds(24 + 2 * outer + k, 1), :]

    group_mask = iota((64, 128), 1) // 32 == iota((64, 128), 0) // 16
    for group in range(8):
        block = jnp.concatenate(
            [x_ref[:, (4 * group + k) * 256 : (4 * group + k + 1) * 256] for k in range(4)], axis=0
        )
        basis = v_ref[4 * group : 4 * group + 4].reshape(128, 256)
        coefs = lax.dot_general(block, basis, (((1,), (1,)), ((), ())), preferred_element_type=F32)
        wide_ref[pl.ds(64 * group, 64), :] = spread(coefs, group_mask, matrix)

    for level in range(5):
        first, after = LEVEL_ROW[level], LEVEL_ROW[level + 1]
        parents = []
        for g in range((after - first) // 2):
            total = None
            for child in (first + 2 * g, first + 2 * g + 1):
                term = apply(wide_ref[pl.ds(16 * child, 16), :], ef_ref[pl.ds(child, 1), :])
                total = term if total is None else total + term
            parents.append(fold(total))
        rows = 16 * len(parents)
        coefs = jnp.concatenate(parents, axis=0) if len(parents) > 1 else parents[0]
        wide_ref[pl.ds(16 * after, rows), :] = spread(coefs, first_group(rows), matrix)
    lift_ref[...] = fold(apply(wide_ref[pl.ds(16 * 62, 16), :], ef_ref[pl.ds(62, 1), :]))

    low_half = iota((8, 128), 1) < 64
    even = (iota((8, 128), 1) // 32) % 2 == 0
    prod_ref[pl.ds(504, 8), :] = jnp.zeros((8, 512), F32)

    @pl.loop(0, 63)
    def _(p):
        couple = b_ref[p].astype(F32)
        for quad in range(4):
            sums = [
                apply(couple, wide_ref[pl.ds(p * 16 + 4 * quad + k, 1), :]) for k in range(4)
            ]
            a0, a1, a2, a3 = sums[2], sums[1], sums[0], sums[3]
            w02 = jnp.where(low_half, a0, a2) + pltpu.roll(jnp.where(low_half, a2, a0), 64, 1)
            w13 = jnp.where(low_half, a1, a3) + pltpu.roll(jnp.where(low_half, a3, a1), 64, 1)
            w20 = pltpu.roll(w02, 64, 1)
            done = jnp.where(even, w20, w13) + pltpu.roll(jnp.where(even, w13, w02), 32, 1)
            prod_ref[pl.ds(p * 8, 8), pl.ds(128 * quad, 128)] = done

    table = lane_ref[...]
    pick = (iota((8, 768), 0) == table[1:2, :]).astype(F32)
    mine = (iota((63, 768), 0) == table[0:1, :]).astype(F32)
    offset = jnp.sum(dot((fd_ref[...] - me + 32).astype(F32), pick) * mine, axis=0, keepdims=True)
    slot = jnp.sum(dot(fs_ref[...].astype(F32), pick) * mine, axis=0, keepdims=True)
    target = table[2:3, :] * (offset.astype(jnp.int32) - 32) + slot.astype(jnp.int32) + table[3:4, :]

    def chosen(rows, start, lanes, high, low):
        hot = jnp.where(iota((rows, lanes), 0) == target[:, start : start + lanes], 1.0, 0.0)
        hot = hot.astype(BF16)
        return dot(hot, high) + dot(hot, low)

    def put(offset, tile, value):
        if offset == 0:
            own_ref[tile] = value
        else:
            send_ref[slot_of(offset) + tile] = value.astype(BF16)

    out = chosen(160, 0, 256, *halves(prod_ref[0:256, :]))
    for k in range(5):
        for half in range(2):
            for j in range(4):
                put(k - 2, 8 + 4 * half + j, out[k * 32 + half * 16 : k * 32 + half * 16 + 16, j * 128 : j * 128 + 128])
    out = chosen(144, 256, 128, *halves(prod_ref[256:384, :]))
    for k in range(9):
        for j in range(4):
            put(k - 4, 4 + j, out[k * 16 : k * 16 + 16, j * 128 : j * 128 + 128])
    part = jnp.concatenate([prod_ref[384:448, j * 256 : j * 256 + 256] for j in range(2)], axis=0)
    out = chosen(272, 384, 128, *halves(part))
    for k in range(17):
        for j in range(2):
            put(k - 8, 2 + j, out[k * 16 : k * 16 + 16, j * 128 : j * 128 + 128])
    part = jnp.concatenate([prod_ref[448:480, j * 128 : j * 128 + 128] for j in range(4)], axis=0)
    out = chosen(528, 512, 128, *halves(part))
    for k in range(33):
        put(k - 16, 1, out[k * 16 : k * 16 + 16, :])
    part = jnp.concatenate([prod_ref[480:512, j * 128 : j * 128 + 128] for j in range(4)], axis=0)
    out = chosen(1040, 640, 128, *halves(part))
    for k in range(65):
        put(k - 32, 0, out[k * 16 : k * 16 + 16, :])


def link_kernel(
    send_ref, own_ref, lift_ref, f_ref, x_ref, rr_ref, near_index, self_hbm, near_hbm,
    sum_ref, upper_ref, near_ref,
    far_ref, shock_ref, lifts_ref, pack_ref, self_v, near_v,
    far_send, far_recv, shock_send, shock_recv, in_send, in_recv, out_send, out_recv, load_sem,
):
    outer = lax.axis_index("outer")
    inner = lax.axis_index("inner")
    me = outer * 8 + inner

    def load(c, kind):
        source, target = (self_hbm, self_v) if kind == 0 else (near_hbm, near_v)
        return pltpu.make_async_copy(
            source.at[pl.ds(4 * c, 4)], target.at[pl.ds(4 * c, 4)], load_sem.at[kind, c]
        )

    def place(index):
        return (lax.div(index, 8), lax.rem(index, 8))

    barrier = pltpu.get_barrier_semaphore()

    @pl.loop(1, 33)
    def _(step):
        pl.semaphore_signal(barrier, inc=1, device_id=place(lax.rem(me + step, 128)), device_id_type=MESH)
        pl.semaphore_signal(barrier, inc=1, device_id=place(lax.rem(me + 128 - step, 128)), device_id_type=MESH)

    @pl.loop(5, 12)
    def _(step):
        pl.semaphore_signal(barrier, inc=1, device_id=(lax.rem(outer + step, 16), inner), device_id_type=MESH)

    for c in range(8):
        for kind in range(2):
            load(c, kind).start()
    for g in range(32):
        shock_ref[32 + g] = x_ref[:, 256 * g : 256 * g + 256]
    shock_ref[96] = jnp.zeros((16, 256), BF16)
    pl.semaphore_wait(barrier, 71)

    def lift_copy(k):
        return pltpu.make_async_remote_copy(
            src_ref=lift_ref,
            dst_ref=lifts_ref.at[inner],
            send_sem=in_send.at[k - 1],
            recv_sem=in_recv.at[k - 1],
            device_id=(outer, lax.rem(inner + k, 8)),
            device_id_type=MESH,
        )

    def pack_copy(k):
        return pltpu.make_async_remote_copy(
            src_ref=pack_ref,
            dst_ref=upper_ref.at[outer],
            send_sem=out_send.at[k - 1],
            recv_sem=out_recv.at[k - 1],
            device_id=(lax.rem(outer + k, 16), inner),
            device_id_type=MESH,
        )

    def shock_copy(k):
        return pltpu.make_async_remote_copy(
            src_ref=shock_ref.at[pl.ds(32, 32)],
            dst_ref=shock_ref.at[pl.ds(64 * k, 32)],
            send_sem=shock_send.at[k],
            recv_sem=shock_recv.at[k],
            device_id=place(lax.rem(me + (1 if k == 0 else 127), 128)),
            device_id_type=MESH,
        )

    def far_copy(number, index):
        near, far, tiles, base = CLASSES[number]
        count = far - near + 1
        offset = jnp.where(index < count, index - far, index - count + near)
        first = sum(2 * (c[1] - c[0] + 1) for c in CLASSES[:number])
        span = pl.ds(base + index * tiles, tiles)
        return pltpu.make_async_remote_copy(
            src_ref=send_ref.at[span],
            dst_ref=far_ref.at[span],
            send_sem=far_send.at[first + index],
            recv_sem=far_recv.at[first + index],
            device_id=place(lax.rem(me + offset + 128, 128)),
            device_id_type=MESH,
        )

    for k in range(1, 8):
        lift_copy(k).start()
    for number in range(5):
        near, far, _, _ = CLASSES[number]

        @pl.loop(0, 2 * (far - near + 1))
        def _(index, number=number):
            far_copy(number, index).start()

    for k in range(2):
        shock_copy(k).start()
    lifts_ref[inner] = lift_ref[...]

    matrix = rr_ref[...]
    for k in range(1, 8):
        lift_copy(k).wait_recv()
    sixth = [lifts_ref[2 * j] + lifts_ref[2 * j + 1] for j in range(4)]
    wide = spread(jnp.concatenate(sixth, axis=0), first_group(64), matrix)
    fifth = [
        fold(
            apply(wide[32 * j : 32 * j + 16], f_ref[2 * j : 2 * j + 1, :])
            + apply(wide[32 * j + 16 : 32 * j + 32], f_ref[2 * j + 1 : 2 * j + 2, :])
        )
        for j in range(2)
    ]
    wide = spread(jnp.concatenate(fifth, axis=0), first_group(32), matrix)
    fourth = fold(apply(wide[0:16], f_ref[4:5, :]) + apply(wide[16:32], f_ref[5:6, :]))
    group = iota((16, 128), 1) // 32
    pack_ref[:, 0:128] = jnp.where(
        group < 2, jnp.where(group == 0, sixth[0], sixth[1]), jnp.where(group == 2, sixth[2], sixth[3])
    )
    pack_ref[:, 128:256] = jnp.where(
        group < 2, jnp.where(group == 0, fifth[0], fifth[1]), jnp.where(group == 2, fourth, 0.0)
    )
    for k in range(1, 16):
        pack_copy(k).start()
    upper_ref[outer] = pack_ref[...]

    for k in range(2):
        shock_copy(k).wait_recv()
    for c in range(8):
        for kind in range(2):
            load(c, kind).wait()

        @pl.loop(4 * c, 4 * c + 4)
        def _(g):
            total = dot(shock_ref[32 + g], self_v[g])
            for j in range(3):
                total = total + dot(shock_ref[near_index[g * 3 + j]], near_v[g, j])
            near_ref[:, pl.ds(pl.multiple_of(g * 256, 256), 256)] = total

    sum_ref[...] = own_ref[...]
    for number in range(5):
        near, far, tiles, base = CLASSES[number]

        @pl.loop(0, 2 * (far - near + 1))
        def _(index, number=number, tiles=tiles, base=base):
            far_copy(number, index).wait_recv()
            for t in range(tiles):
                sum_ref[t] = sum_ref[t] + far_ref[base + index * tiles + t].astype(F32)

    for k in range(1, 16):
        pack_copy(k).wait_recv()
    for k in range(1, 8):
        lift_copy(k).wait_send()
    for k in range(1, 16):
        pack_copy(k).wait_send()
    for k in range(2):
        shock_copy(k).wait_send()
    for number in range(5):
        near, far, _, _ = CLASSES[number]

        @pl.loop(0, 2 * (far - near + 1))
        def _(index, number=number):
            far_copy(number, index).wait_send()


def down_kernel(
    sum_ref, upper_ref, near_ref, v_ref, e_ref, ut_ref, rr_ref, gather_ref, select_ref, partner_ref, uc_hbm,
    out_ref,
    ef_ref, uf_ref, couple_ref, wide4_ref, wide3_ref, wide2_ref, lhs_ref, wide56_ref, inject_ref, local_ref,
    high_ref, low_ref, sem,
):
    outer = lax.axis_index("outer")
    me = outer * 8 + lax.axis_index("inner")
    nodes = [lax.div(128 + me, 2 ** (7 - level)) for level in range(2, 7)]
    loads = [
        pltpu.make_async_copy(uc_hbm.at[nodes[k] - 4], couple_ref.at[k], sem.at[k]) for k in range(5)
    ]
    for copy in loads:
        copy.start()
    matrix = rr_ref[...]
    gather = gather_ref[...]
    ef_ref[pl.ds(0, 63), :] = e_ref[...].astype(F32)
    uf_ref[...] = ut_ref[...].astype(F32)

    mask = iota((256, 128), 1) // 32 == 2
    wide4_ref[...] = spread(upper_ref[:, :, 128:256].reshape(256, 128), mask, matrix).reshape(16, 16, 1024)

    def parents(wide_ref, count, first):
        made = []
        for g in range(count):
            total = apply(wide_ref[2 * g], uf_ref[pl.ds(first + 2 * g, 1), :])
            total = total + apply(wide_ref[2 * g + 1], uf_ref[pl.ds(first + 2 * g + 1, 1), :])
            made.append(fold(total))
        return spread(jnp.concatenate(made, axis=0), first_group(16 * count), matrix).reshape(count, 16, 1024)

    wide3_ref[...] = parents(wide4_ref, 8, 8)
    wide2_ref[...] = parents(wide3_ref, 4, 0)

    lane_group = iota((16, 128), 1) // 32
    for f in range(8):
        node = partner_ref[nodes[4] - 4, f] - 64
        piece = upper_ref[lax.div(node, 4), :, 0:128]
        lhs_ref[pl.ds(16 * f, 16), :] = jnp.where(lane_group == lax.rem(node, 4), piece, 0.0)
        node = partner_ref[nodes[3] - 4, f] - 32
        piece = upper_ref[lax.div(node, 2), :, 128:256]
        lhs_ref[pl.ds(128 + 16 * f, 16), :] = jnp.where(lane_group == lax.rem(node, 2), piece, 0.0)
    high, low = halves(lhs_ref[...])
    wide56_ref[...] = dot(jnp.concatenate([high, low], axis=1), matrix).reshape(16, 16, 1024)
    for copy in loads:
        copy.wait()
    fields = []
    for k in range(5):
        couple = couple_ref[k].astype(F32)
        total = None
        for f in range(8):
            if k == 4:
                wide = wide56_ref[f]
            elif k == 3:
                wide = wide56_ref[8 + f]
            else:
                base, ref = ((4, wide2_ref), (8, wide3_ref), (16, wide4_ref))[k]
                wide = ref[partner_ref[nodes[k] - 4, f] - base]
            term = apply(wide, couple[f : f + 1, :])
            total = term if total is None else total + term
        fields.append(fold(total))

    half_mask = [iota((8, 128), 0) == 4 * a + iota((8, 128), 1) // 32 for a in range(2)]

    def source(p, j, a):
        if p < 32:
            return sum_ref[8 + 4 * (p // 16) + 2 * j + a, p % 16 : p % 16 + 1, :]
        if p < 48:
            return sum_ref[4 + 2 * j + a, p - 32 : p - 31, :]
        if p < 56:
            return sum_ref[2 + a, j * 8 + p - 48 : j * 8 + p - 47, :]
        row = (2 * j + a) * 4
        if p < 60:
            return sum_ref[1, row + p - 56 : row + p - 55, :]
        return sum_ref[0, row + p - 60 : row + p - 59, :]

    for p in range(63):
        for j in range(2):
            for a in range(2):
                inject_ref[pl.ds(16 * p + 8 * j, 8), 128 * a : 128 * a + 128] = jnp.where(
                    half_mask[a], source(p, j, a), 0.0
                )
    high, low = halves(inject_ref[...])
    local_ref[...] = dot(high, select_ref[...]) + dot(low, select_ref[...])

    def turn(field, row):
        return jnp.concatenate([field * row[:, t * 128 : t * 128 + 128] for t in range(8)], axis=1)

    def step(field, row):
        high, low = halves(turn(field, row))
        both = dot(jnp.concatenate([high, low], axis=0), gather)
        return both[0:16] + both[16:32]

    down = fields[0]
    for k in range(1, 5):
        down = fields[k] + step(down, uf_ref[pl.ds(nodes[k] - 8, 1), :])
    current = local_ref[pl.ds(16 * 62, 16), :] + step(down, ef_ref[pl.ds(62, 1), :])
    for level in range(4, -1, -1):
        first, after = LEVEL_ROW[level], LEVEL_ROW[level + 1]
        for c in range(after - first):
            parent = current[16 * (c // 2) : 16 * (c // 2) + 16]
            high, low = halves(turn(parent, ef_ref[pl.ds(first + c, 1), :]))
            high_ref[pl.ds(16 * c, 16), :] = high
            low_ref[pl.ds(16 * c, 16), :] = low
        rows = 16 * (after - first)
        current = (
            local_ref[pl.ds(16 * first, rows), :]
            + dot(high_ref[pl.ds(0, rows), :], gather)
            + dot(low_ref[pl.ds(0, rows), :], gather)
        )

    group_mask = iota((64, 128), 1) // 32 == iota((64, 128), 0) // 16
    for group in range(8):
        high, low = halves(jnp.where(group_mask, current[64 * group : 64 * group + 64], 0.0))
        basis = v_ref[4 * group : 4 * group + 4].reshape(128, 256)
        both = dot(jnp.concatenate([high, low], axis=0), basis)
        both = both[0:64] + both[64:128]
        for k in range(4):
            lanes = pl.ds((4 * group + k) * 256, 256)
            out_ref[:, lanes] = near_ref[:, lanes] + both[16 * k : 16 * k + 16]


def local(
    shocks,
    leaf_basis,
    self_block,
    near_block,
    near_offset,
    near_count,
    local_transfer,
    local_coupling,
    far_device,
    far_slot,
    upper_transfer,
    upper_coupling,
    upper_partner,
):
    matrix = jnp.asarray(SPREAD, BF16)
    me = lax.axis_index("outer") * 8 + lax.axis_index("inner")
    near_index = jnp.arange(32, dtype=jnp.int32)[:, None] + near_offset + 32
    source = me * 32 - 32 + near_index
    live = jnp.arange(3, dtype=jnp.int32)[None, :] < near_count[:, None]
    live = live & (source >= 0) & (source < 4096)
    near_index = jnp.where(live, near_index, 96).reshape(96)
    shape = jax.ShapeDtypeStruct
    limit = 56 * 2**20
    send, own, lift, links = pl.pallas_call(
        up_kernel,
        out_shape=(
            shape((TILES, 16, 128), BF16),
            shape((16, 16, 128), F32),
            shape((16, 128), F32),
            shape((8, 1024), F32),
        ),
        in_specs=[VMEM] * 9,
        out_specs=(VMEM,) * 4,
        scratch_shapes=[
            pltpu.VMEM((64, 1024), F32),
            pltpu.VMEM((120, 1024), F32),
            pltpu.VMEM((1008, 1024), F32),
            pltpu.VMEM((512, 512), F32),
        ],
        compiler_params=pltpu.CompilerParams(vmem_limit_bytes=limit),
        name="up",
    )(
        shocks, leaf_basis, local_transfer, local_coupling, far_device, far_slot, upper_transfer, matrix,
        jnp.asarray(LANES),
    )
    sums, upper, near = pl.pallas_call(
        link_kernel,
        out_shape=(
            shape((16, 16, 128), F32),
            shape((16, 16, 256), F32),
            shape((16, 8192), F32),
        ),
        in_specs=[VMEM] * 6 + [SMEM] + [ANY] * 2,
        out_specs=(VMEM,) * 3,
        scratch_shapes=[
            pltpu.VMEM((TILES, 16, 128), BF16),
            pltpu.VMEM((97, 16, 256), BF16),
            pltpu.VMEM((8, 16, 128), F32),
            pltpu.VMEM((16, 256), F32),
            pltpu.VMEM((32, 256, 256), BF16),
            pltpu.VMEM((32, 3, 256, 256), BF16),
            pltpu.SemaphoreType.DMA((MESSAGES,)),
            pltpu.SemaphoreType.DMA((MESSAGES,)),
            pltpu.SemaphoreType.DMA((2,)),
            pltpu.SemaphoreType.DMA((2,)),
            pltpu.SemaphoreType.DMA((7,)),
            pltpu.SemaphoreType.DMA((7,)),
            pltpu.SemaphoreType.DMA((15,)),
            pltpu.SemaphoreType.DMA((15,)),
            pltpu.SemaphoreType.DMA((2, 8)),
        ],
        compiler_params=pltpu.CompilerParams(
            vmem_limit_bytes=limit, collective_id=0, has_side_effects=True
        ),
        name="link",
    )(send, own, lift, links, shocks, matrix, near_index, self_block, near_block)
    return pl.pallas_call(
        down_kernel,
        out_shape=shape((16, 8192), F32),
        in_specs=[VMEM] * 9 + [SMEM, ANY],
        out_specs=VMEM,
        scratch_shapes=[
            pltpu.VMEM((64, 1024), F32),
            pltpu.VMEM((120, 1024), F32),
            pltpu.VMEM((5, 8, 1024), BF16),
            pltpu.VMEM((16, 16, 1024), F32),
            pltpu.VMEM((8, 16, 1024), F32),
            pltpu.VMEM((4, 16, 1024), F32),
            pltpu.VMEM((256, 128), F32),
            pltpu.VMEM((16, 16, 1024), F32),
            pltpu.VMEM((1008, 256), F32),
            pltpu.VMEM((1008, 128), F32),
            pltpu.VMEM((512, 1024), BF16),
            pltpu.VMEM((512, 1024), BF16),
            pltpu.SemaphoreType.DMA((5,)),
        ],
        compiler_params=pltpu.CompilerParams(vmem_limit_bytes=limit),
        name="down",
    )(
        sums, upper, near, leaf_basis, local_transfer, upper_transfer, matrix, jnp.asarray(GATHER, BF16),
        jnp.asarray(SELECT, BF16), upper_partner, upper_coupling,
    )


def solution(mesh):
    both = ("outer", "inner")
    placed = (
        P(None, both),
        P(both, None, None),
        P(both, None, None),
        P(both, None, None, None),
        P(both, None),
        P(both),
        P(both, None),
        P(both, None, None),
        P(both, None),
        P(both, None),
        P(),
        P(),
        P(),
    )
    return jax.shard_map(
        local, mesh=mesh, in_specs=placed, out_specs=P(None, both), check_vma=False
    )
```

```python
import jax
import jax.numpy as jnp
import numpy as np
from jax import lax
from jax.experimental import pallas as pl
from jax.experimental.pallas import tpu as pltpu
from jax.sharding import PartitionSpec as P

F32 = jnp.float32
BF16 = jnp.bfloat16
MESH = pl.DeviceIdType.MESH
VMEM = pl.BlockSpec(memory_space=pltpu.VMEM)
SMEM = pl.BlockSpec(memory_space=pltpu.SMEM)
ANY = pl.BlockSpec(memory_space=pl.ANY)

CLASSES = ((1, 2, 16, 0), (3, 4, 8, 64), (5, 8, 4, 96), (9, 16, 2, 128), (17, 32, 1, 160))
TILES = 192


def slot_of(offset):
    for near, far, tiles, base in CLASSES:
        if near <= abs(offset) <= far:
            count = far - near + 1
            place = offset + far if offset < 0 else offset - near + count
            return base + place * tiles
    return None


LEVEL_ROW = (0, 32, 48, 56, 60, 62, 63)


def lane_table():
    table = np.zeros((8, 768), np.int32)
    for lane in range(768):
        if lane < 256:
            item, part, scale, shift = lane, 0, 32, 64
        elif lane < 384:
            item, part, scale, shift = lane, 0, 16, 64 - 32
        elif lane < 512:
            item, part = 384 + (lane - 384) % 64, (lane - 384) // 64
            scale, shift = 16, 128 + 8 * part - 48
        elif lane < 640:
            item, part = 448 + (lane - 512) % 32, (lane - 512) // 32
            scale, shift = 16, 256 + 4 * part - 56
        else:
            item, part = 480 + (lane - 640) % 32, (lane - 640) // 32
            scale, shift = 16, 512 + 4 * part - 60
        if item >= 504:
            scale, shift = 0, -1000000
        table[0, lane], table[1, lane], table[2, lane], table[3, lane] = item // 8, item % 8, scale, shift
    return table


LANES = lane_table()

def iota(shape, dim):
    return lax.broadcasted_iota(jnp.int32, shape, dim)


def halves(x):
    high = x.astype(BF16)
    low = (x - high.astype(F32)).astype(BF16)
    return high, low


def dot(a, b):
    return jnp.dot(a, b, preferred_element_type=F32)


def spread(coefs, mask, matrix):
    high, low = halves(jnp.where(mask, coefs, 0.0))
    return dot(jnp.concatenate([high, low], axis=1), matrix)


def fold(x):
    x = x + pltpu.roll(x, 64, 1)
    return x + pltpu.roll(x, 32, 1)


def apply(wide, row):
    total = wide[:, 0:128] * row[:, 0:128]
    for t in range(1, 8):
        total = total + wide[:, t * 128 : t * 128 + 128] * row[:, t * 128 : t * 128 + 128]
    return total


def first_group(rows):
    return iota((rows, 128), 1) < 32


def kernel(
    x_ref, v_ref, e_ref, ut_ref, fd_ref, fs_ref, lane_ref, off_ref, count_ref, partner_ref,
    b_hbm, uc_hbm, self_hbm, near_hbm,
    out_ref,
    b_ref, self_v, near_v, couple_ref, ef_ref, uf_ref, wide_ref, prod_ref, spread_ref, gather_ref, select_ref,
    send_ref, far_ref, sum_ref, shock_ref, lift_ref, lifts_ref, pack_ref, upper_ref,
    index_v, index_s, node_ref, top_ref, wide56_ref,
    inject_ref, local_ref, high_ref, low_ref,
    load_sem, couple_sem, index_sem, far_send, far_recv, shock_send, shock_recv, in_send, in_recv,
    out_send, out_recv,
):
    outer = lax.axis_index("outer")
    inner = lax.axis_index("inner")
    me = outer * 8 + inner
    nodes = [lax.div(128 + me, 2 ** (7 - level)) for level in range(2, 7)]

    def place(index):
        return (lax.div(index, 8), lax.rem(index, 8))

    def load_basis():
        return pltpu.make_async_copy(b_hbm, b_ref.at[pl.ds(0, 63)], load_sem.at[2, 0])

    def load_upper(k):
        return pltpu.make_async_copy(uc_hbm.at[nodes[k] - 4], couple_ref.at[k], couple_sem.at[k])

    def load(c, kind):
        source, target = (self_hbm, self_v) if kind == 0 else (near_hbm, near_v)
        return pltpu.make_async_copy(
            source.at[pl.ds(4 * c, 4)], target.at[pl.ds(4 * c, 4)], load_sem.at[kind, c]
        )

    load_basis().start()
    for k in range(5):
        load_upper(k).start()
    for c in range(8):
        for kind in range(2):
            load(c, kind).start()

    barrier = pltpu.get_barrier_semaphore()

    @pl.loop(1, 33)
    def _(step):
        pl.semaphore_signal(barrier, inc=1, device_id=place(lax.rem(me + step, 128)), device_id_type=MESH)
        pl.semaphore_signal(barrier, inc=1, device_id=place(lax.rem(me + 128 - step, 128)), device_id_type=MESH)

    @pl.loop(5, 12)
    def _(step):
        pl.semaphore_signal(barrier, inc=1, device_id=(lax.rem(outer + step, 16), inner), device_id_type=MESH)

    unit = jnp.where(iota((32, 1024), 0) == iota((32, 1024), 1) // 32, 1.0, 0.0).astype(BF16)
    for k in range(8):
        spread_ref[32 * k : 32 * k + 32, :] = unit
    gather_ref[...] = jnp.where(iota((1024, 128), 0) // 32 == iota((1024, 128), 1) % 32, 1.0, 0.0).astype(BF16)
    unit = jnp.where(iota((32, 128), 0) == iota((32, 128), 1) % 32, 1.0, 0.0).astype(BF16)
    for k in range(8):
        select_ref[32 * k : 32 * k + 32, :] = unit

    near_row = iota((3, 32), 1) + off_ref[...] + 32
    source = me * 32 - 32 + near_row
    live = (iota((3, 32), 0) < count_ref[...]) & (source >= 0) & (source < 4096)
    index_v[...] = jnp.zeros((8, 128), jnp.int32)
    index_v[0:3, 0:32] = jnp.where(live, near_row, 96)
    index_copy = pltpu.make_async_copy(index_v, index_s, index_sem)
    index_copy.start()
    for g in range(32):
        shock_ref[32 + g] = x_ref[:, 256 * g : 256 * g + 256]
    shock_ref[96] = jnp.zeros((16, 256), BF16)
    ef_ref[pl.ds(0, 63), :] = e_ref[...].astype(F32)
    uf_ref[...] = ut_ref[...].astype(F32)
    matrix = spread_ref[...]

    group_mask = iota((64, 128), 1) // 32 == iota((64, 128), 0) // 16
    for group in range(8):
        block = shock_ref[32 + 4 * group : 36 + 4 * group].reshape(64, 256)
        basis = v_ref[4 * group : 4 * group + 4].reshape(128, 256)
        coefs = lax.dot_general(block, basis, (((1,), (1,)), ((), ())), preferred_element_type=F32)
        wide_ref[pl.ds(64 * group, 64), :] = spread(coefs, group_mask, matrix)

    for level in range(5):
        first, after = LEVEL_ROW[level], LEVEL_ROW[level + 1]
        parents = []
        for g in range((after - first) // 2):
            total = None
            for child in (first + 2 * g, first + 2 * g + 1):
                term = apply(wide_ref[pl.ds(16 * child, 16), :], ef_ref[pl.ds(child, 1), :])
                total = term if total is None else total + term
            parents.append(fold(total))
        rows = 16 * len(parents)
        coefs = jnp.concatenate(parents, axis=0) if len(parents) > 1 else parents[0]
        wide_ref[pl.ds(16 * after, rows), :] = spread(coefs, first_group(rows), matrix)
    lift_ref[...] = fold(apply(wide_ref[pl.ds(16 * 62, 16), :], ef_ref[pl.ds(62, 1), :]))

    def lift_copy(k):
        return pltpu.make_async_remote_copy(
            src_ref=lift_ref,
            dst_ref=lifts_ref.at[inner],
            send_sem=in_send,
            recv_sem=in_recv,
            device_id=(outer, lax.rem(inner + k, 8)),
            device_id_type=MESH,
        )

    def pack_copy(k):
        return pltpu.make_async_remote_copy(
            src_ref=pack_ref,
            dst_ref=upper_ref.at[outer],
            send_sem=out_send,
            recv_sem=out_recv,
            device_id=(lax.rem(outer + k, 16), inner),
            device_id_type=MESH,
        )

    def shock_copy(k):
        return pltpu.make_async_remote_copy(
            src_ref=shock_ref.at[pl.ds(32, 32)],
            dst_ref=shock_ref.at[pl.ds(64 * k, 32)],
            send_sem=shock_send.at[k],
            recv_sem=shock_recv.at[k],
            device_id=place(lax.rem(me + (1 if k == 0 else 127), 128)),
            device_id_type=MESH,
        )

    def far_start(number):
        near, far, tiles, base = CLASSES[number]
        count = far - near + 1

        @pl.loop(0, 2 * count)
        def _(index):
            offset = jnp.where(index < count, index - far, index - count + near)
            span = pl.ds(base + index * tiles, tiles)
            pltpu.make_async_remote_copy(
                src_ref=send_ref.at[span],
                dst_ref=far_ref.at[span],
                send_sem=far_send.at[number],
                recv_sem=far_recv.at[number],
                device_id=place(lax.rem(me + offset + 128, 128)),
                device_id_type=MESH,
            ).start()

    def wait_all(ref, sem):
        pltpu.make_async_copy(ref, ref, sem).wait()

    def far_part(ref, number):
        near, far, tiles, base = CLASSES[number]
        return ref.at[pl.ds(base, 2 * (far - near + 1) * tiles)]

    pl.semaphore_wait(barrier, 71)
    for k in range(1, 8):
        lift_copy(k).start()
    for k in range(2):
        shock_copy(k).start()
    lifts_ref[inner] = lift_ref[...]

    table = lane_ref[...]
    pick = (iota((8, 768), 0) == table[1:2, :]).astype(F32)
    mine = (iota((63, 768), 0) == table[0:1, :]).astype(F32)
    offset = jnp.sum(dot((fd_ref[...] - me + 32).astype(F32), mine) * pick, axis=0, keepdims=True)
    slot = jnp.sum(dot(fs_ref[...].astype(F32), mine) * pick, axis=0, keepdims=True)
    target = table[2:3, :] * (offset.astype(jnp.int32) - 32) + slot.astype(jnp.int32) + table[3:4, :]

    low_half = iota((8, 128), 1) < 64
    even = (iota((8, 128), 1) // 32) % 2 == 0

    def couple(start, stop):
        @pl.loop(start, stop, unroll=8)
        def _(p):
            blocks = b_ref[p].astype(F32)
            for quad in range(4):
                sums = [apply(blocks, wide_ref[pl.ds(p * 16 + 4 * quad + k, 1), :]) for k in range(4)]
                a0, a1, a2, a3 = sums[2], sums[1], sums[0], sums[3]
                w02 = jnp.where(low_half, a0, a2) + pltpu.roll(jnp.where(low_half, a2, a0), 64, 1)
                w13 = jnp.where(low_half, a1, a3) + pltpu.roll(jnp.where(low_half, a3, a1), 64, 1)
                w20 = pltpu.roll(w02, 64, 1)
                done = jnp.where(even, w20, w13) + pltpu.roll(jnp.where(even, w13, w02), 32, 1)
                prod_ref[pl.ds(p * 8, 8), pl.ds(128 * quad, 128)] = done

    def chosen(rows, start, lanes, high, low):
        hot = jnp.where(iota((rows, lanes), 0) == target[:, start : start + lanes], 1.0, 0.0)
        hot = hot.astype(BF16)
        return dot(hot, high) + dot(hot, low)

    def put(offset, tile, value):
        if offset == 0:
            sum_ref[tile] = value
        else:
            send_ref[slot_of(offset) + tile] = value.astype(BF16)

    wide_ref[1008:1024, :] = jnp.zeros((16, 1024), F32)
    load_basis().wait()
    b_ref[63] = jnp.zeros((8, 1024), BF16)
    couple(32, 64)
    part = jnp.concatenate([prod_ref[480:512, j * 128 : j * 128 + 128] for j in range(4)], axis=0)
    out = chosen(1040, 640, 128, *halves(part))
    for k in range(65):
        put(k - 32, 0, out[k * 16 : k * 16 + 16, :])
    far_start(4)
    part = jnp.concatenate([prod_ref[448:480, j * 128 : j * 128 + 128] for j in range(4)], axis=0)
    out = chosen(528, 512, 128, *halves(part))
    for k in range(33):
        put(k - 16, 1, out[k * 16 : k * 16 + 16, :])
    far_start(3)
    part = jnp.concatenate([prod_ref[384:448, j * 256 : j * 256 + 256] for j in range(2)], axis=0)
    out = chosen(272, 384, 128, *halves(part))
    for k in range(17):
        for j in range(2):
            put(k - 8, 2 + j, out[k * 16 : k * 16 + 16, j * 128 : j * 128 + 128])
    far_start(2)
    out = chosen(144, 256, 128, *halves(prod_ref[256:384, :]))
    for k in range(9):
        for j in range(4):
            put(k - 4, 4 + j, out[k * 16 : k * 16 + 16, j * 128 : j * 128 + 128])
    far_start(1)

    wait_all(lifts_ref.at[pl.ds(0, 7)], in_recv)
    sixth = [lifts_ref[2 * j] + lifts_ref[2 * j + 1] for j in range(4)]
    wide = spread(jnp.concatenate(sixth, axis=0), first_group(64), matrix)

    def link(first, k):
        return uf_ref[pl.ds(first + k, 1), :]

    fifth = [
        fold(
            apply(wide[32 * j : 32 * j + 16], link(56 + 4 * outer, 2 * j))
            + apply(wide[32 * j + 16 : 32 * j + 32], link(56 + 4 * outer, 2 * j + 1))
        )
        for j in range(2)
    ]
    wide = spread(jnp.concatenate(fifth, axis=0), first_group(32), matrix)
    fourth = fold(apply(wide[0:16], link(24 + 2 * outer, 0)) + apply(wide[16:32], link(24 + 2 * outer, 1)))
    group = iota((16, 128), 1) // 32
    pack_ref[:, 0:128] = jnp.where(
        group < 2, jnp.where(group == 0, sixth[0], sixth[1]), jnp.where(group == 2, sixth[2], sixth[3])
    )
    pack_ref[:, 128:256] = jnp.where(
        group < 2, jnp.where(group == 0, fifth[0], fifth[1]), jnp.where(group == 2, fourth, 0.0)
    )
    for k in range(1, 16):
        pack_copy(k).start()
    upper_ref[outer] = pack_ref[...]

    couple(0, 32)
    out = chosen(160, 0, 256, *halves(prod_ref[0:256, :]))
    for k in range(5):
        for half in range(2):
            for j in range(4):
                row = k * 32 + half * 16
                put(k - 2, 8 + 4 * half + j, out[row : row + 16, j * 128 : j * 128 + 128])
    far_start(0)

    index_copy.wait()
    for k in range(2):
        shock_copy(k).wait_recv()
    for c in range(8):
        for kind in range(2):
            load(c, kind).wait()

        @pl.loop(4 * c, 4 * c + 4, unroll=2)
        def _(g):
            total = dot(shock_ref[32 + g], self_v[g])
            for j in range(3):
                total = total + dot(shock_ref[index_s[j, g]], near_v[g, j])
            out_ref[:, pl.ds(pl.multiple_of(g * 256, 256), 256)] = total

    wait_all(upper_ref.at[pl.ds(0, 15)], out_recv)
    mask = iota((256, 128), 1) // 32 == 2
    node_ref[0] = jnp.zeros((16, 128), F32)
    top_ref[0] = jnp.zeros((16, 1024), F32)
    top_ref[16:32] = spread(upper_ref[:, :, 128:256].reshape(256, 128), mask, matrix).reshape(16, 16, 1024)
    for k in range(16):
        for j in range(4):
            node_ref[64 + 4 * k + j] = jnp.where(group == j, upper_ref[k, :, 0:128], 0.0)
        for j in range(2):
            node_ref[32 + 2 * k + j] = jnp.where(group == j, upper_ref[k, :, 128:256], 0.0)

    def parents(count):
        made = []
        for g in range(count, 2 * count):
            total = apply(top_ref[2 * g], uf_ref[pl.ds(2 * g - 8, 1), :])
            total = total + apply(top_ref[2 * g + 1], uf_ref[pl.ds(2 * g - 7, 1), :])
            made.append(fold(total))
        wide = spread(jnp.concatenate(made, axis=0), first_group(16 * count), matrix)
        top_ref[count : 2 * count] = wide.reshape(count, 16, 1024)

    parents(8)
    parents(4)

    rows = [node_ref[partner_ref[f, nodes[k] - 4]] for k in (4, 3) for f in range(8)]
    high, low = halves(jnp.concatenate(rows, axis=0))
    wide56_ref[...] = dot(jnp.concatenate([high, low], axis=1), matrix).reshape(16, 16, 1024)
    fields = []
    for k in range(5):
        load_upper(k).wait()
        blocks = couple_ref[k].astype(F32)
        total = None
        for f in range(8):
            if k == 4:
                wide = wide56_ref[f]
            elif k == 3:
                wide = wide56_ref[8 + f]
            else:
                wide = top_ref[partner_ref[f, nodes[k] - 4]]
            term = apply(wide, blocks[f : f + 1, :])
            total = term if total is None else total + term
        fields.append(fold(total))

    gather = gather_ref[...]

    def turn(field, row):
        return jnp.concatenate([field * row[:, t * 128 : t * 128 + 128] for t in range(8)], axis=1)

    def step(field, row):
        high, low = halves(turn(field, row))
        both = dot(jnp.concatenate([high, low], axis=0), gather)
        return both[0:16] + both[16:32]

    down = fields[0]
    for k in range(1, 5):
        down = fields[k] + step(down, uf_ref[pl.ds(nodes[k] - 8, 1), :])
    current = step(down, ef_ref[pl.ds(62, 1), :])

    for number in (4, 3, 2, 1, 0):
        near, far, tiles, base = CLASSES[number]
        count = 2 * (far - near + 1)
        wait_all(far_part(far_ref, number), far_recv.at[number])
        for t in range(tiles):
            total = sum_ref[t]
            for k in range(count):
                total = total + far_ref[base + k * tiles + t].astype(F32)
            sum_ref[t] = total

    half_mask = [iota((8, 128), 0) == 4 * a + iota((8, 128), 1) // 32 for a in range(2)]

    def source_row(p, j, a):
        if p < 32:
            return sum_ref[8 + 4 * (p // 16) + 2 * j + a, p % 16 : p % 16 + 1, :]
        if p < 48:
            return sum_ref[4 + 2 * j + a, p - 32 : p - 31, :]
        if p < 56:
            return sum_ref[2 + a, j * 8 + p - 48 : j * 8 + p - 47, :]
        row = (2 * j + a) * 4
        if p < 60:
            return sum_ref[1, row + p - 56 : row + p - 55, :]
        return sum_ref[0, row + p - 60 : row + p - 59, :]

    for p in range(63):
        for j in range(2):
            for a in range(2):
                inject_ref[pl.ds(16 * p + 8 * j, 8), 128 * a : 128 * a + 128] = jnp.where(
                    half_mask[a], source_row(p, j, a), 0.0
                )
    high, low = halves(inject_ref[...])
    local_ref[...] = dot(high, select_ref[...]) + dot(low, select_ref[...])

    current = current + local_ref[pl.ds(16 * 62, 16), :]
    for level in range(4, -1, -1):
        first, after = LEVEL_ROW[level], LEVEL_ROW[level + 1]
        for c in range(after - first):
            parent = current[16 * (c // 2) : 16 * (c // 2) + 16]
            high, low = halves(turn(parent, ef_ref[pl.ds(first + c, 1), :]))
            high_ref[pl.ds(16 * c, 16), :] = high
            low_ref[pl.ds(16 * c, 16), :] = low
        rows = 16 * (after - first)
        current = (
            local_ref[pl.ds(16 * first, rows), :]
            + dot(high_ref[pl.ds(0, rows), :], gather)
            + dot(low_ref[pl.ds(0, rows), :], gather)
        )

    for group in range(8):
        high, low = halves(jnp.where(group_mask, current[64 * group : 64 * group + 64], 0.0))
        basis = v_ref[4 * group : 4 * group + 4].reshape(128, 256)
        both = dot(jnp.concatenate([high, low], axis=0), basis)
        both = both[0:64] + both[64:128]
        for k in range(4):
            lanes = pl.ds((4 * group + k) * 256, 256)
            out_ref[:, lanes] = out_ref[:, lanes] + both[16 * k : 16 * k + 16]

    wait_all(lifts_ref.at[pl.ds(0, 7)], in_send)
    wait_all(upper_ref.at[pl.ds(0, 15)], out_send)
    for k in range(2):
        shock_copy(k).wait_send()
    for number in range(5):
        wait_all(far_part(send_ref, number), far_send.at[number])


def local(
    shocks,
    leaf_basis,
    self_block,
    near_block,
    near_offset,
    near_count,
    local_transfer,
    local_coupling,
    far_device,
    far_slot,
    upper_transfer,
    upper_coupling,
    upper_partner,
):
    return pl.pallas_call(
        kernel,
        out_shape=jax.ShapeDtypeStruct((16, 8192), F32),
        in_specs=[VMEM] * 9 + [SMEM] + [ANY] * 4,
        out_specs=VMEM,
        scratch_shapes=[
            pltpu.VMEM((64, 8, 1024), BF16),
            pltpu.VMEM((32, 256, 256), BF16),
            pltpu.VMEM((32, 3, 256, 256), BF16),
            pltpu.VMEM((5, 8, 1024), BF16),
            pltpu.VMEM((64, 1024), F32),
            pltpu.VMEM((120, 1024), F32),
            pltpu.VMEM((1024, 1024), F32),
            pltpu.VMEM((512, 512), F32),
            pltpu.VMEM((256, 1024), BF16),
            pltpu.VMEM((1024, 128), BF16),
            pltpu.VMEM((256, 128), BF16),
            pltpu.VMEM((TILES, 16, 128), BF16),
            pltpu.VMEM((TILES, 16, 128), BF16),
            pltpu.VMEM((16, 16, 128), F32),
            pltpu.VMEM((97, 16, 256), BF16),
            pltpu.VMEM((16, 128), F32),
            pltpu.VMEM((8, 16, 128), F32),
            pltpu.VMEM((16, 256), F32),
            pltpu.VMEM((16, 16, 256), F32),
            pltpu.VMEM((8, 128), jnp.int32),
            pltpu.SMEM((8, 128), jnp.int32),
            pltpu.VMEM((128, 16, 128), F32),
            pltpu.VMEM((32, 16, 1024), F32),
            pltpu.VMEM((16, 16, 1024), F32),
            pltpu.VMEM((1008, 256), F32),
            pltpu.VMEM((1008, 128), F32),
            pltpu.VMEM((512, 1024), BF16),
            pltpu.VMEM((512, 1024), BF16),
            pltpu.SemaphoreType.DMA((3, 8)),
            pltpu.SemaphoreType.DMA((5,)),
            pltpu.SemaphoreType.DMA,
            pltpu.SemaphoreType.DMA((5,)),
            pltpu.SemaphoreType.DMA((5,)),
            pltpu.SemaphoreType.DMA((2,)),
            pltpu.SemaphoreType.DMA((2,)),
            pltpu.SemaphoreType.DMA,
            pltpu.SemaphoreType.DMA,
            pltpu.SemaphoreType.DMA,
            pltpu.SemaphoreType.DMA,
        ],
        compiler_params=pltpu.CompilerParams(
            vmem_limit_bytes=56 * 2**20, collective_id=0, has_side_effects=True
        ),
        name="whole",
    )(
        shocks, leaf_basis, local_transfer, upper_transfer, far_device.T, far_slot.T, jnp.asarray(LANES),
        near_offset.T, near_count.reshape(1, 32), upper_partner.T, local_coupling, upper_coupling,
        self_block, near_block,
    )


def solution(mesh):
    both = ("outer", "inner")
    placed = (
        P(None, both),
        P(both, None, None),
        P(both, None, None),
        P(both, None, None, None),
        P(both, None),
        P(both),
        P(both, None),
        P(both, None, None),
        P(both, None),
        P(both, None),
        P(),
        P(),
        P(),
    )
    return jax.shard_map(
        local, mesh=mesh, in_specs=placed, out_specs=P(None, both), check_vma=False
    )
```

```python
import jax
import jax.numpy as jnp
import numpy as np
from jax import lax
from jax.experimental import pallas as pl
from jax.experimental.pallas import tpu as pltpu
from jax.sharding import PartitionSpec as P

F32 = jnp.float32
BF16 = jnp.bfloat16
MESH = pl.DeviceIdType.MESH
VMEM = pl.BlockSpec(memory_space=pltpu.VMEM)
SMEM = pl.BlockSpec(memory_space=pltpu.SMEM)
ANY = pl.BlockSpec(memory_space=pl.ANY)

CLASSES = ((1, 2, 16, 0), (3, 4, 8, 64), (5, 8, 4, 96), (9, 16, 2, 128), (17, 32, 1, 160))
TILES = 192


def slot_of(offset):
    for near, far, tiles, base in CLASSES:
        if near <= abs(offset) <= far:
            count = far - near + 1
            place = offset + far if offset < 0 else offset - near + count
            return base + place * tiles
    return None


LEVEL_ROW = (0, 32, 48, 56, 60, 62, 63)


def lane_table():
    table = np.zeros((8, 768), np.int32)
    for lane in range(768):
        if lane < 256:
            item, part, scale, shift = lane, 0, 32, 64
        elif lane < 384:
            item, part, scale, shift = lane, 0, 16, 64 - 32
        elif lane < 512:
            item, part = 384 + (lane - 384) % 64, (lane - 384) // 64
            scale, shift = 16, 128 + 8 * part - 48
        elif lane < 640:
            item, part = 448 + (lane - 512) % 32, (lane - 512) // 32
            scale, shift = 16, 256 + 4 * part - 56
        else:
            item, part = 480 + (lane - 640) % 32, (lane - 640) // 32
            scale, shift = 16, 512 + 4 * part - 60
        if item >= 504:
            scale, shift = 0, -1000000
        table[0, lane], table[1, lane], table[2, lane], table[3, lane] = item // 8, item % 8, scale, shift
    return table


LANES = lane_table()

def iota(shape, dim):
    return lax.broadcasted_iota(jnp.int32, shape, dim)


def halves(x):
    high = x.astype(BF16)
    low = (x - high.astype(F32)).astype(BF16)
    return high, low


def dot(a, b):
    return jnp.dot(a, b, preferred_element_type=F32)


def spread(coefs, mask, matrix):
    high, low = halves(jnp.where(mask, coefs, 0.0))
    return dot(jnp.concatenate([high, low], axis=1), matrix)


def fold(x):
    x = x + pltpu.roll(x, 64, 1)
    return x + pltpu.roll(x, 32, 1)


def apply(wide, row):
    total = wide[:, 0:128] * row[:, 0:128]
    for t in range(1, 8):
        total = total + wide[:, t * 128 : t * 128 + 128] * row[:, t * 128 : t * 128 + 128]
    return total


def first_group(rows):
    return iota((rows, 128), 1) < 32


def kernel(
    x_ref, v_ref, e_ref, ut_ref, fd_ref, fs_ref, lane_ref, off_ref, count_ref, partner_ref,
    b_hbm, uc_hbm, self_hbm, near_hbm,
    out_ref,
    b_ref, self_v, near_v, couple_ref, ef_ref, uf_ref, wide_ref, prod_ref, spread_ref, gather_ref, select_ref,
    send_ref, far_ref, sum_ref, shock_ref, lift_ref, lifts_ref, pack_ref, upper_ref,
    index_v, index_s, node_ref, top_ref, wide56_ref,
    inject_ref, local_ref, high_ref, low_ref,
    load_sem, couple_sem, index_sem, far_send, far_recv, shock_send, shock_recv, in_send, in_recv,
    out_send, out_recv,
):
    outer = lax.axis_index("outer")
    inner = lax.axis_index("inner")
    me = outer * 8 + inner
    nodes = [lax.div(128 + me, 2 ** (7 - level)) for level in range(2, 7)]

    def place(index):
        return (lax.div(index, 8), lax.rem(index, 8))

    def load_basis():
        return pltpu.make_async_copy(b_hbm, b_ref.at[pl.ds(0, 63)], load_sem.at[2, 0])

    def load_upper(k):
        return pltpu.make_async_copy(uc_hbm.at[nodes[k] - 4], couple_ref.at[k], couple_sem.at[k])

    def load(c, kind):
        source, target = (self_hbm, self_v) if kind == 0 else (near_hbm, near_v)
        return pltpu.make_async_copy(
            source.at[pl.ds(4 * c, 4)], target.at[pl.ds(4 * c, 4)], load_sem.at[kind, c]
        )

    load_basis().start()
    for k in range(5):
        load_upper(k).start()
    for c in range(8):
        for kind in range(2):
            load(c, kind).start()

    barrier = pltpu.get_barrier_semaphore()

    @pl.loop(1, 33)
    def _(step):
        pl.semaphore_signal(barrier, inc=1, device_id=place(lax.rem(me + step, 128)), device_id_type=MESH)
        pl.semaphore_signal(barrier, inc=1, device_id=place(lax.rem(me + 128 - step, 128)), device_id_type=MESH)

    @pl.loop(5, 12)
    def _(step):
        pl.semaphore_signal(barrier, inc=1, device_id=(lax.rem(outer + step, 16), inner), device_id_type=MESH)

    unit = jnp.where(iota((32, 1024), 0) == iota((32, 1024), 1) // 32, 1.0, 0.0).astype(BF16)
    for k in range(8):
        spread_ref[32 * k : 32 * k + 32, :] = unit
    gather_ref[...] = jnp.where(iota((1024, 128), 0) // 32 == iota((1024, 128), 1) % 32, 1.0, 0.0).astype(BF16)
    unit = jnp.where(iota((32, 128), 0) == iota((32, 128), 1) % 32, 1.0, 0.0).astype(BF16)
    for k in range(8):
        select_ref[32 * k : 32 * k + 32, :] = unit

    near_row = iota((3, 32), 1) + off_ref[...] + 32
    source = me * 32 - 32 + near_row
    live = (iota((3, 32), 0) < count_ref[...]) & (source >= 0) & (source < 4096)
    index_v[...] = jnp.zeros((8, 128), jnp.int32)
    index_v[0:3, 0:32] = jnp.where(live, near_row, 96)
    index_copy = pltpu.make_async_copy(index_v, index_s, index_sem)
    index_copy.start()
    for g in range(32):
        shock_ref[32 + g] = x_ref[:, 256 * g : 256 * g + 256]
    shock_ref[96] = jnp.zeros((16, 256), BF16)
    ef_ref[pl.ds(0, 63), :] = e_ref[...].astype(F32)
    uf_ref[...] = ut_ref[...].astype(F32)
    matrix = spread_ref[...]

    group_mask = iota((64, 128), 1) // 32 == iota((64, 128), 0) // 16
    for group in range(8):
        block = shock_ref[32 + 4 * group : 36 + 4 * group].reshape(64, 256)
        basis = v_ref[4 * group : 4 * group + 4].reshape(128, 256)
        coefs = lax.dot_general(block, basis, (((1,), (1,)), ((), ())), preferred_element_type=F32)
        wide_ref[pl.ds(64 * group, 64), :] = spread(coefs, group_mask, matrix)

    for level in range(5):
        first, after = LEVEL_ROW[level], LEVEL_ROW[level + 1]
        parents = []
        for g in range((after - first) // 2):
            total = None
            for child in (first + 2 * g, first + 2 * g + 1):
                term = apply(wide_ref[pl.ds(16 * child, 16), :], ef_ref[pl.ds(child, 1), :])
                total = term if total is None else total + term
            parents.append(fold(total))
        rows = 16 * len(parents)
        coefs = jnp.concatenate(parents, axis=0) if len(parents) > 1 else parents[0]
        wide_ref[pl.ds(16 * after, rows), :] = spread(coefs, first_group(rows), matrix)
    lift_ref[...] = fold(apply(wide_ref[pl.ds(16 * 62, 16), :], ef_ref[pl.ds(62, 1), :]))

    def lift_copy(k):
        return pltpu.make_async_remote_copy(
            src_ref=lift_ref,
            dst_ref=lifts_ref.at[inner],
            send_sem=in_send,
            recv_sem=in_recv,
            device_id=(outer, lax.rem(inner + k, 8)),
            device_id_type=MESH,
        )

    def pack_copy(k):
        return pltpu.make_async_remote_copy(
            src_ref=pack_ref,
            dst_ref=upper_ref.at[outer],
            send_sem=out_send,
            recv_sem=out_recv,
            device_id=(lax.rem(outer + k, 16), inner),
            device_id_type=MESH,
        )

    def shock_copy(k):
        return pltpu.make_async_remote_copy(
            src_ref=shock_ref.at[pl.ds(32, 32)],
            dst_ref=shock_ref.at[pl.ds(64 * k, 32)],
            send_sem=shock_send.at[k],
            recv_sem=shock_recv.at[k],
            device_id=place(lax.rem(me + (1 if k == 0 else 127), 128)),
            device_id_type=MESH,
        )

    def far_start(number):
        near, far, tiles, base = CLASSES[number]
        count = far - near + 1

        @pl.loop(0, 2 * count)
        def _(index):
            offset = jnp.where(index < count, index - far, index - count + near)
            span = pl.ds(base + index * tiles, tiles)
            pltpu.make_async_remote_copy(
                src_ref=send_ref.at[span],
                dst_ref=far_ref.at[span],
                send_sem=far_send.at[number],
                recv_sem=far_recv.at[number],
                device_id=place(lax.rem(me + offset + 128, 128)),
                device_id_type=MESH,
            ).start()

    def wait_all(ref, sem):
        pltpu.make_async_copy(ref, ref, sem).wait()

    def far_part(ref, number):
        near, far, tiles, base = CLASSES[number]
        return ref.at[pl.ds(base, 2 * (far - near + 1) * tiles)]

    pl.semaphore_wait(barrier, 71)
    for k in range(1, 8):
        lift_copy(k).start()
    for k in range(2):
        shock_copy(k).start()
    lifts_ref[inner] = lift_ref[...]

    table = lane_ref[...]
    pick = (iota((8, 768), 0) == table[1:2, :]).astype(F32)
    mine = (iota((63, 768), 0) == table[0:1, :]).astype(F32)
    offset = jnp.sum(dot((fd_ref[...] - me + 32).astype(F32), mine) * pick, axis=0, keepdims=True)
    slot = jnp.sum(dot(fs_ref[...].astype(F32), mine) * pick, axis=0, keepdims=True)
    target = table[2:3, :] * (offset.astype(jnp.int32) - 32) + slot.astype(jnp.int32) + table[3:4, :]

    low_half = iota((8, 128), 1) < 64
    even = (iota((8, 128), 1) // 32) % 2 == 0

    def couple(start, stop):
        @pl.loop(start, stop, unroll=8)
        def _(p):
            blocks = b_ref[p].astype(F32)
            for quad in range(4):
                sums = [apply(blocks, wide_ref[pl.ds(p * 16 + 4 * quad + k, 1), :]) for k in range(4)]
                a0, a1, a2, a3 = sums[2], sums[1], sums[0], sums[3]
                w02 = jnp.where(low_half, a0, a2) + pltpu.roll(jnp.where(low_half, a2, a0), 64, 1)
                w13 = jnp.where(low_half, a1, a3) + pltpu.roll(jnp.where(low_half, a3, a1), 64, 1)
                w20 = pltpu.roll(w02, 64, 1)
                done = jnp.where(even, w20, w13) + pltpu.roll(jnp.where(even, w13, w02), 32, 1)
                prod_ref[pl.ds(p * 8, 8), pl.ds(128 * quad, 128)] = done

    def chosen(rows, start, lanes, high, low):
        hot = jnp.where(iota((rows, lanes), 0) == target[:, start : start + lanes], 1.0, 0.0)
        hot = hot.astype(BF16)
        return dot(hot, high) + dot(hot, low)

    def put(offset, tile, value):
        if offset == 0:
            sum_ref[tile] = value
        else:
            send_ref[slot_of(offset) + tile] = value.astype(BF16)

    wide_ref[1008:1024, :] = jnp.zeros((16, 1024), F32)
    load_basis().wait()
    b_ref[63] = jnp.zeros((8, 1024), BF16)
    couple(32, 64)
    wait_all(lifts_ref.at[pl.ds(0, 7)], in_recv)
    sixth = [lifts_ref[2 * j] + lifts_ref[2 * j + 1] for j in range(4)]
    wide = spread(jnp.concatenate(sixth, axis=0), first_group(64), matrix)

    def link(first, k):
        return uf_ref[pl.ds(first + k, 1), :]

    fifth = [
        fold(
            apply(wide[32 * j : 32 * j + 16], link(56 + 4 * outer, 2 * j))
            + apply(wide[32 * j + 16 : 32 * j + 32], link(56 + 4 * outer, 2 * j + 1))
        )
        for j in range(2)
    ]
    wide = spread(jnp.concatenate(fifth, axis=0), first_group(32), matrix)
    fourth = fold(apply(wide[0:16], link(24 + 2 * outer, 0)) + apply(wide[16:32], link(24 + 2 * outer, 1)))
    group = iota((16, 128), 1) // 32
    pack_ref[:, 0:128] = jnp.where(
        group < 2, jnp.where(group == 0, sixth[0], sixth[1]), jnp.where(group == 2, sixth[2], sixth[3])
    ).astype(BF16)
    pack_ref[:, 128:256] = jnp.where(
        group < 2, jnp.where(group == 0, fifth[0], fifth[1]), jnp.where(group == 2, fourth, 0.0)
    ).astype(BF16)
    for k in range(1, 16):
        pack_copy(k).start()
    upper_ref[outer] = pack_ref[...]

    part = jnp.concatenate([prod_ref[480:512, j * 128 : j * 128 + 128] for j in range(4)], axis=0)
    out = chosen(1040, 640, 128, *halves(part))
    for k in range(65):
        put(k - 32, 0, out[k * 16 : k * 16 + 16, :])
    far_start(4)
    part = jnp.concatenate([prod_ref[448:480, j * 128 : j * 128 + 128] for j in range(4)], axis=0)
    out = chosen(528, 512, 128, *halves(part))
    for k in range(33):
        put(k - 16, 1, out[k * 16 : k * 16 + 16, :])
    far_start(3)
    part = jnp.concatenate([prod_ref[384:448, j * 256 : j * 256 + 256] for j in range(2)], axis=0)
    out = chosen(272, 384, 128, *halves(part))
    for k in range(17):
        for j in range(2):
            put(k - 8, 2 + j, out[k * 16 : k * 16 + 16, j * 128 : j * 128 + 128])
    far_start(2)
    out = chosen(144, 256, 128, *halves(prod_ref[256:384, :]))
    for k in range(9):
        for j in range(4):
            put(k - 4, 4 + j, out[k * 16 : k * 16 + 16, j * 128 : j * 128 + 128])
    far_start(1)

    couple(0, 32)
    out = chosen(160, 0, 256, *halves(prod_ref[0:256, :]))
    for k in range(5):
        for half in range(2):
            for j in range(4):
                row = k * 32 + half * 16
                put(k - 2, 8 + 4 * half + j, out[row : row + 16, j * 128 : j * 128 + 128])
    far_start(0)

    index_copy.wait()
    for k in range(2):
        shock_copy(k).wait_recv()
    for c in range(8):
        for kind in range(2):
            load(c, kind).wait()

        @pl.loop(4 * c, 4 * c + 4, unroll=2)
        def _(g):
            total = dot(shock_ref[32 + g], self_v[g])
            for j in range(3):
                total = total + dot(shock_ref[index_s[j, g]], near_v[g, j])
            out_ref[:, pl.ds(pl.multiple_of(g * 256, 256), 256)] = total

    wait_all(upper_ref.at[pl.ds(0, 15)], out_recv)
    mask = iota((256, 128), 1) // 32 == 2
    node_ref[0] = jnp.zeros((16, 128), BF16)
    top_ref[0] = jnp.zeros((16, 1024), F32)
    coefs = jnp.where(mask, upper_ref[:, :, 128:256].reshape(256, 128).astype(F32), 0.0).astype(BF16)
    top_ref[16:32] = dot(coefs, spread_ref[0:128, :]).reshape(16, 16, 1024)
    for k in range(16):
        for j in range(4):
            node_ref[64 + 4 * k + j] = jnp.where(group == j, upper_ref[k, :, 0:128].astype(F32), 0.0).astype(BF16)
        for j in range(2):
            node_ref[32 + 2 * k + j] = jnp.where(group == j, upper_ref[k, :, 128:256].astype(F32), 0.0).astype(BF16)

    def parents(count):
        made = []
        for g in range(count, 2 * count):
            total = apply(top_ref[2 * g], uf_ref[pl.ds(2 * g - 8, 1), :])
            total = total + apply(top_ref[2 * g + 1], uf_ref[pl.ds(2 * g - 7, 1), :])
            made.append(fold(total))
        wide = spread(jnp.concatenate(made, axis=0), first_group(16 * count), matrix)
        top_ref[count : 2 * count] = wide.reshape(count, 16, 1024)

    parents(8)
    parents(4)

    rows = [node_ref[partner_ref[f, nodes[k] - 4]] for k in (4, 3) for f in range(8)]
    wide56_ref[...] = dot(jnp.concatenate(rows, axis=0), spread_ref[0:128, :]).reshape(16, 16, 1024)
    fields = []
    for k in range(5):
        load_upper(k).wait()
        blocks = couple_ref[k].astype(F32)
        total = None
        for f in range(8):
            if k == 4:
                wide = wide56_ref[f]
            elif k == 3:
                wide = wide56_ref[8 + f]
            else:
                wide = top_ref[partner_ref[f, nodes[k] - 4]]
            term = apply(wide, blocks[f : f + 1, :])
            total = term if total is None else total + term
        fields.append(fold(total))

    gather = gather_ref[...]

    def turn(field, row):
        return jnp.concatenate([field * row[:, t * 128 : t * 128 + 128] for t in range(8)], axis=1)

    def step(field, row):
        high, low = halves(turn(field, row))
        both = dot(jnp.concatenate([high, low], axis=0), gather)
        return both[0:16] + both[16:32]

    down = fields[0]
    for k in range(1, 5):
        down = fields[k] + step(down, uf_ref[pl.ds(nodes[k] - 8, 1), :])
    current = step(down, ef_ref[pl.ds(62, 1), :])

    for number in (4, 3, 2, 1, 0):
        near, far, tiles, base = CLASSES[number]
        count = 2 * (far - near + 1)
        wait_all(far_part(far_ref, number), far_recv.at[number])
        for t in range(tiles):
            total = sum_ref[t]
            for k in range(count):
                total = total + far_ref[base + k * tiles + t].astype(F32)
            sum_ref[t] = total

    half_mask = [iota((8, 128), 0) == 4 * a + iota((8, 128), 1) // 32 for a in range(2)]

    def source_row(p, j, a):
        if p < 32:
            return sum_ref[8 + 4 * (p // 16) + 2 * j + a, p % 16 : p % 16 + 1, :]
        if p < 48:
            return sum_ref[4 + 2 * j + a, p - 32 : p - 31, :]
        if p < 56:
            return sum_ref[2 + a, j * 8 + p - 48 : j * 8 + p - 47, :]
        row = (2 * j + a) * 4
        if p < 60:
            return sum_ref[1, row + p - 56 : row + p - 55, :]
        return sum_ref[0, row + p - 60 : row + p - 59, :]

    for p in range(63):
        for j in range(2):
            for a in range(2):
                inject_ref[pl.ds(16 * p + 8 * j, 8), 128 * a : 128 * a + 128] = jnp.where(
                    half_mask[a], source_row(p, j, a), 0.0
                )
    high, low = halves(inject_ref[...])
    local_ref[...] = dot(high, select_ref[...]) + dot(low, select_ref[...])

    current = current + local_ref[pl.ds(16 * 62, 16), :]
    for level in range(4, -1, -1):
        first, after = LEVEL_ROW[level], LEVEL_ROW[level + 1]
        for c in range(after - first):
            parent = current[16 * (c // 2) : 16 * (c // 2) + 16]
            high, low = halves(turn(parent, ef_ref[pl.ds(first + c, 1), :]))
            high_ref[pl.ds(16 * c, 16), :] = high
            low_ref[pl.ds(16 * c, 16), :] = low
        rows = 16 * (after - first)
        current = (
            local_ref[pl.ds(16 * first, rows), :]
            + dot(high_ref[pl.ds(0, rows), :], gather)
            + dot(low_ref[pl.ds(0, rows), :], gather)
        )

    for group in range(8):
        high, low = halves(jnp.where(group_mask, current[64 * group : 64 * group + 64], 0.0))
        basis = v_ref[4 * group : 4 * group + 4].reshape(128, 256)
        both = dot(jnp.concatenate([high, low], axis=0), basis)
        both = both[0:64] + both[64:128]
        for k in range(4):
            lanes = pl.ds((4 * group + k) * 256, 256)
            out_ref[:, lanes] = out_ref[:, lanes] + both[16 * k : 16 * k + 16]

    wait_all(lifts_ref.at[pl.ds(0, 7)], in_send)
    wait_all(upper_ref.at[pl.ds(0, 15)], out_send)
    for k in range(2):
        shock_copy(k).wait_send()
    for number in range(5):
        wait_all(far_part(send_ref, number), far_send.at[number])


def local(
    shocks,
    leaf_basis,
    self_block,
    near_block,
    near_offset,
    near_count,
    local_transfer,
    local_coupling,
    far_device,
    far_slot,
    upper_transfer,
    upper_coupling,
    upper_partner,
):
    return pl.pallas_call(
        kernel,
        out_shape=jax.ShapeDtypeStruct((16, 8192), F32),
        in_specs=[VMEM] * 9 + [SMEM] + [ANY] * 4,
        out_specs=VMEM,
        scratch_shapes=[
            pltpu.VMEM((64, 8, 1024), BF16),
            pltpu.VMEM((32, 256, 256), BF16),
            pltpu.VMEM((32, 3, 256, 256), BF16),
            pltpu.VMEM((5, 8, 1024), BF16),
            pltpu.VMEM((64, 1024), F32),
            pltpu.VMEM((120, 1024), F32),
            pltpu.VMEM((1024, 1024), F32),
            pltpu.VMEM((512, 512), F32),
            pltpu.VMEM((256, 1024), BF16),
            pltpu.VMEM((1024, 128), BF16),
            pltpu.VMEM((256, 128), BF16),
            pltpu.VMEM((TILES, 16, 128), BF16),
            pltpu.VMEM((TILES, 16, 128), BF16),
            pltpu.VMEM((16, 16, 128), F32),
            pltpu.VMEM((97, 16, 256), BF16),
            pltpu.VMEM((16, 128), F32),
            pltpu.VMEM((8, 16, 128), F32),
            pltpu.VMEM((16, 256), BF16),
            pltpu.VMEM((16, 16, 256), BF16),
            pltpu.VMEM((8, 128), jnp.int32),
            pltpu.SMEM((8, 128), jnp.int32),
            pltpu.VMEM((128, 16, 128), BF16),
            pltpu.VMEM((32, 16, 1024), F32),
            pltpu.VMEM((16, 16, 1024), F32),
            pltpu.VMEM((1008, 256), F32),
            pltpu.VMEM((1008, 128), F32),
            pltpu.VMEM((512, 1024), BF16),
            pltpu.VMEM((512, 1024), BF16),
            pltpu.SemaphoreType.DMA((3, 8)),
            pltpu.SemaphoreType.DMA((5,)),
            pltpu.SemaphoreType.DMA,
            pltpu.SemaphoreType.DMA((5,)),
            pltpu.SemaphoreType.DMA((5,)),
            pltpu.SemaphoreType.DMA((2,)),
            pltpu.SemaphoreType.DMA((2,)),
            pltpu.SemaphoreType.DMA,
            pltpu.SemaphoreType.DMA,
            pltpu.SemaphoreType.DMA,
            pltpu.SemaphoreType.DMA,
        ],
        compiler_params=pltpu.CompilerParams(
            vmem_limit_bytes=56 * 2**20, collective_id=0, has_side_effects=True
        ),
        name="whole",
    )(
        shocks, leaf_basis, local_transfer, upper_transfer, far_device.T, far_slot.T, jnp.asarray(LANES),
        near_offset.T, near_count.reshape(1, 32), upper_partner.T, local_coupling, upper_coupling,
        self_block, near_block,
    )


def solution(mesh):
    both = ("outer", "inner")
    placed = (
        P(None, both),
        P(both, None, None),
        P(both, None, None),
        P(both, None, None, None),
        P(both, None),
        P(both),
        P(both, None),
        P(both, None, None),
        P(both, None),
        P(both, None),
        P(),
        P(),
        P(),
    )
    return jax.shard_map(
        local, mesh=mesh, in_specs=placed, out_specs=P(None, both), check_vma=False
    )
```

```python
import jax
import jax.numpy as jnp
import numpy as np
from jax import lax
from jax.experimental import pallas as pl
from jax.experimental.pallas import tpu as pltpu
from jax.sharding import PartitionSpec as P

F32 = jnp.float32
BF16 = jnp.bfloat16
MESH = pl.DeviceIdType.MESH
VMEM = pl.BlockSpec(memory_space=pltpu.VMEM)
SMEM = pl.BlockSpec(memory_space=pltpu.SMEM)
ANY = pl.BlockSpec(memory_space=pl.ANY)

CLASSES = ((1, 2, 16, 0), (3, 4, 8, 64), (5, 8, 4, 96), (9, 16, 2, 128), (17, 32, 1, 160))
TILES = 192


def slot_of(offset):
    for near, far, tiles, base in CLASSES:
        if near <= abs(offset) <= far:
            count = far - near + 1
            place = offset + far if offset < 0 else offset - near + count
            return base + place * tiles
    return None


LEVEL_ROW = (0, 32, 48, 56, 60, 62, 63)


def lane_table():
    table = np.zeros((8, 768), np.int32)
    for lane in range(768):
        if lane < 256:
            item, part, scale, shift = lane, 0, 32, 64
        elif lane < 384:
            item, part, scale, shift = lane, 0, 16, 64 - 32
        elif lane < 512:
            item, part = 384 + (lane - 384) % 64, (lane - 384) // 64
            scale, shift = 16, 128 + 8 * part - 48
        elif lane < 640:
            item, part = 448 + (lane - 512) % 32, (lane - 512) // 32
            scale, shift = 16, 256 + 4 * part - 56
        else:
            item, part = 480 + (lane - 640) % 32, (lane - 640) // 32
            scale, shift = 16, 512 + 4 * part - 60
        if item >= 504:
            scale, shift = 0, -1000000
        table[0, lane], table[1, lane], table[2, lane], table[3, lane] = item // 8, item % 8, scale, shift
    return table


LANES = lane_table()

def iota(shape, dim):
    return lax.broadcasted_iota(jnp.int32, shape, dim)


def halves(x):
    high = x.astype(BF16)
    low = (x - high.astype(F32)).astype(BF16)
    return high, low


def dot(a, b):
    return jnp.dot(a, b, preferred_element_type=F32)


def spread(coefs, mask, matrix):
    high, low = halves(jnp.where(mask, coefs, 0.0))
    return dot(jnp.concatenate([high, low], axis=1), matrix)


def fold(x):
    x = x + pltpu.roll(x, 64, 1)
    return x + pltpu.roll(x, 32, 1)


def apply(wide, row):
    total = wide[:, 0:128] * row[:, 0:128]
    for t in range(1, 8):
        total = total + wide[:, t * 128 : t * 128 + 128] * row[:, t * 128 : t * 128 + 128]
    return total


def first_group(rows):
    return iota((rows, 128), 1) < 32


def kernel(
    x_ref, v_ref, e_ref, ut_ref, fd_ref, fs_ref, lane_ref, off_ref, count_ref, partner_ref,
    b_hbm, uc_hbm, self_hbm, near_hbm,
    out_ref,
    b_ref, self_v, near_v, couple_ref, ef_ref, uf_ref, wide_ref, prod_ref, spread_ref, gather_ref, select_ref,
    send_ref, far_ref, sum_ref, shock_ref, lift_ref, lifts_ref, pack_ref, upper_ref,
    index_v, index_s, node_ref, top_ref, wide56_ref,
    inject_ref, local_ref, high_ref, low_ref, near_ref, stack_ref,
    load_sem, couple_sem, index_sem, far_send, far_recv, shock_send, shock_recv, in_send, in_recv,
    out_send, out_recv,
):
    outer = lax.axis_index("outer")
    inner = lax.axis_index("inner")
    me = outer * 8 + inner
    nodes = [lax.div(128 + me, 2 ** (7 - level)) for level in range(2, 7)]

    def place(index):
        return (lax.div(index, 8), lax.rem(index, 8))

    def load_basis():
        return pltpu.make_async_copy(b_hbm, b_ref.at[pl.ds(0, 63)], load_sem.at[2, 0])

    def load_upper(k):
        return pltpu.make_async_copy(uc_hbm.at[nodes[k] - 4], couple_ref.at[k], couple_sem.at[k])

    def load(c, kind):
        source, target = (self_hbm, self_v) if kind == 0 else (near_hbm, near_v)
        return pltpu.make_async_copy(
            source.at[pl.ds(4 * c, 4)], target.at[pl.ds(4 * c, 4)], load_sem.at[kind, c]
        )

    barrier = pltpu.get_barrier_semaphore()

    @pl.loop(1, 33)
    def _(step):
        pl.semaphore_signal(barrier, inc=1, device_id=place(lax.rem(me + step, 128)), device_id_type=MESH)
        pl.semaphore_signal(barrier, inc=1, device_id=place(lax.rem(me + 128 - step, 128)), device_id_type=MESH)

    @pl.loop(5, 12)
    def _(step):
        pl.semaphore_signal(barrier, inc=1, device_id=(lax.rem(outer + step, 16), inner), device_id_type=MESH)

    load_basis().start()
    for k in range(5):
        load_upper(k).start()
    for c in range(8):
        for kind in range(2):
            load(c, kind).start()

    unit = jnp.where(iota((32, 1024), 0) == iota((32, 1024), 1) // 32, 1.0, 0.0).astype(BF16)
    for k in range(8):
        spread_ref[32 * k : 32 * k + 32, :] = unit
    gather_ref[...] = jnp.where(iota((1024, 128), 0) // 32 == iota((1024, 128), 1) % 32, 1.0, 0.0).astype(BF16)
    unit = jnp.where(iota((32, 128), 0) == iota((32, 128), 1) % 32, 1.0, 0.0).astype(BF16)
    for k in range(8):
        select_ref[32 * k : 32 * k + 32, :] = unit

    near_row = iota((3, 32), 1) + off_ref[...] + 32
    source = me * 32 - 32 + near_row
    live = (iota((3, 32), 0) < count_ref[...]) & (source >= 0) & (source < 4096)
    index_v[...] = jnp.zeros((8, 128), jnp.int32)
    index_v[0:3, 0:32] = jnp.where(live, near_row, 96)
    index_copy = pltpu.make_async_copy(index_v, index_s, index_sem)
    index_copy.start()
    for g in range(32):
        shock_ref[32 + g] = x_ref[:, 256 * g : 256 * g + 256]
    shock_ref[96] = jnp.zeros((16, 256), BF16)
    ef_ref[pl.ds(0, 63), :] = e_ref[...].astype(F32)
    uf_ref[...] = ut_ref[...].astype(F32)
    matrix = spread_ref[...]

    group_mask = iota((64, 128), 1) // 32 == iota((64, 128), 0) // 16
    for group in range(8):
        block = shock_ref[32 + 4 * group : 36 + 4 * group].reshape(64, 256)
        basis = v_ref[4 * group : 4 * group + 4].reshape(128, 256)
        coefs = lax.dot_general(block, basis, (((1,), (1,)), ((), ())), preferred_element_type=F32)
        wide_ref[pl.ds(64 * group, 64), :] = spread(coefs, group_mask, matrix)

    for level in range(5):
        first, after = LEVEL_ROW[level], LEVEL_ROW[level + 1]
        parents = []
        for g in range((after - first) // 2):
            total = None
            for child in (first + 2 * g, first + 2 * g + 1):
                term = apply(wide_ref[pl.ds(16 * child, 16), :], ef_ref[pl.ds(child, 1), :])
                total = term if total is None else total + term
            parents.append(fold(total))
        rows = 16 * len(parents)
        coefs = jnp.concatenate(parents, axis=0) if len(parents) > 1 else parents[0]
        wide_ref[pl.ds(16 * after, rows), :] = spread(coefs, first_group(rows), matrix)
    lift_ref[...] = fold(apply(wide_ref[pl.ds(16 * 62, 16), :], ef_ref[pl.ds(62, 1), :]))

    def lift_copy(k):
        return pltpu.make_async_remote_copy(
            src_ref=lift_ref,
            dst_ref=lifts_ref.at[inner],
            send_sem=in_send,
            recv_sem=in_recv,
            device_id=(outer, lax.rem(inner + k, 8)),
            device_id_type=MESH,
        )

    def pack_copy(k):
        return pltpu.make_async_remote_copy(
            src_ref=pack_ref,
            dst_ref=upper_ref.at[outer],
            send_sem=out_send,
            recv_sem=out_recv,
            device_id=(lax.rem(outer + k, 16), inner),
            device_id_type=MESH,
        )

    def shock_copy(k):
        return pltpu.make_async_remote_copy(
            src_ref=shock_ref.at[pl.ds(32, 32)],
            dst_ref=shock_ref.at[pl.ds(64 * k, 32)],
            send_sem=shock_send.at[k],
            recv_sem=shock_recv.at[k],
            device_id=place(lax.rem(me + (1 if k == 0 else 127), 128)),
            device_id_type=MESH,
        )

    def far_start(number):
        near, far, tiles, base = CLASSES[number]
        count = far - near + 1

        @pl.loop(0, 2 * count)
        def _(index):
            offset = jnp.where(index < count, index - far, index - count + near)
            span = pl.ds(base + index * tiles, tiles)
            pltpu.make_async_remote_copy(
                src_ref=send_ref.at[span],
                dst_ref=far_ref.at[span],
                send_sem=far_send.at[number],
                recv_sem=far_recv.at[number],
                device_id=place(lax.rem(me + offset + 128, 128)),
                device_id_type=MESH,
            ).start()

    def wait_all(ref, sem):
        pltpu.make_async_copy(ref, ref, sem).wait()

    def far_part(ref, number):
        near, far, tiles, base = CLASSES[number]
        return ref.at[pl.ds(base, 2 * (far - near + 1) * tiles)]

    pl.semaphore_wait(barrier, 71)
    for k in range(1, 8):
        lift_copy(k).start()
    for k in range(2):
        shock_copy(k).start()
    lifts_ref[inner] = lift_ref[...]

    table = lane_ref[...]
    pick = (iota((8, 768), 0) == table[1:2, :]).astype(F32)
    mine = (iota((63, 768), 0) == table[0:1, :]).astype(F32)
    offset = jnp.sum(dot((fd_ref[...] - me + 32).astype(F32), mine) * pick, axis=0, keepdims=True)
    slot = jnp.sum(dot(fs_ref[...].astype(F32), mine) * pick, axis=0, keepdims=True)
    target = table[2:3, :] * (offset.astype(jnp.int32) - 32) + slot.astype(jnp.int32) + table[3:4, :]

    low_half = iota((8, 128), 1) < 64
    even = (iota((8, 128), 1) // 32) % 2 == 0

    def couple(start, stop):
        @pl.loop(start, stop, unroll=8)
        def _(p):
            blocks = b_ref[p].astype(F32)
            for quad in range(4):
                sums = [apply(blocks, wide_ref[pl.ds(p * 16 + 4 * quad + k, 1), :]) for k in range(4)]
                a0, a1, a2, a3 = sums[2], sums[1], sums[0], sums[3]
                w02 = jnp.where(low_half, a0, a2) + pltpu.roll(jnp.where(low_half, a2, a0), 64, 1)
                w13 = jnp.where(low_half, a1, a3) + pltpu.roll(jnp.where(low_half, a3, a1), 64, 1)
                w20 = pltpu.roll(w02, 64, 1)
                done = jnp.where(even, w20, w13) + pltpu.roll(jnp.where(even, w13, w02), 32, 1)
                prod_ref[pl.ds(p * 8, 8), pl.ds(128 * quad, 128)] = done

    def chosen(rows, start, lanes, high, low):
        hot = jnp.where(iota((rows, lanes), 0) == target[:, start : start + lanes], 1.0, 0.0)
        hot = hot.astype(BF16)
        return dot(hot, high) + dot(hot, low)

    def put(offset, tile, value):
        if offset == 0:
            sum_ref[tile] = value
        else:
            send_ref[slot_of(offset) + tile] = value.astype(BF16)

    wide_ref[1008:1024, :] = jnp.zeros((16, 1024), F32)
    load_basis().wait()
    b_ref[63] = jnp.zeros((8, 1024), BF16)
    couple(32, 64)
    wait_all(lifts_ref.at[pl.ds(0, 7)], in_recv)
    sixth = [lifts_ref[2 * j] + lifts_ref[2 * j + 1] for j in range(4)]
    wide = spread(jnp.concatenate(sixth, axis=0), first_group(64), matrix)

    def link(first, k):
        return uf_ref[pl.ds(first + k, 1), :]

    fifth = [
        fold(
            apply(wide[32 * j : 32 * j + 16], link(56 + 4 * outer, 2 * j))
            + apply(wide[32 * j + 16 : 32 * j + 32], link(56 + 4 * outer, 2 * j + 1))
        )
        for j in range(2)
    ]
    wide = spread(jnp.concatenate(fifth, axis=0), first_group(32), matrix)
    fourth = fold(apply(wide[0:16], link(24 + 2 * outer, 0)) + apply(wide[16:32], link(24 + 2 * outer, 1)))
    group = iota((16, 128), 1) // 32
    pack_ref[:, 0:128] = jnp.where(
        group < 2, jnp.where(group == 0, sixth[0], sixth[1]), jnp.where(group == 2, sixth[2], sixth[3])
    ).astype(BF16)
    pack_ref[:, 128:256] = jnp.where(
        group < 2, jnp.where(group == 0, fifth[0], fifth[1]), jnp.where(group == 2, fourth, 0.0)
    ).astype(BF16)
    for k in range(1, 16):
        pack_copy(k).start()
    upper_ref[outer] = pack_ref[...]

    part = jnp.concatenate([prod_ref[480:512, j * 128 : j * 128 + 128] for j in range(4)], axis=0)
    out = chosen(1040, 640, 128, *halves(part))
    for k in range(65):
        put(k - 32, 0, out[k * 16 : k * 16 + 16, :])
    far_start(4)
    part = jnp.concatenate([prod_ref[448:480, j * 128 : j * 128 + 128] for j in range(4)], axis=0)
    out = chosen(528, 512, 128, *halves(part))
    for k in range(33):
        put(k - 16, 1, out[k * 16 : k * 16 + 16, :])
    far_start(3)
    part = jnp.concatenate([prod_ref[384:448, j * 256 : j * 256 + 256] for j in range(2)], axis=0)
    out = chosen(272, 384, 128, *halves(part))
    for k in range(17):
        for j in range(2):
            put(k - 8, 2 + j, out[k * 16 : k * 16 + 16, j * 128 : j * 128 + 128])
    far_start(2)
    out = chosen(144, 256, 128, *halves(prod_ref[256:384, :]))
    for k in range(9):
        for j in range(4):
            put(k - 4, 4 + j, out[k * 16 : k * 16 + 16, j * 128 : j * 128 + 128])
    far_start(1)

    couple(0, 32)
    out = chosen(160, 0, 256, *halves(prod_ref[0:256, :]))
    for k in range(5):
        for half in range(2):
            for j in range(4):
                row = k * 32 + half * 16
                put(k - 2, 8 + 4 * half + j, out[row : row + 16, j * 128 : j * 128 + 128])
    far_start(0)

    spot = iota((32, 1024), 1) // 32 == iota((32, 1024), 0)
    unit = jnp.where(iota((1024, 128), 0) % 32 == iota((1024, 128), 1) % 32, 1.0, 0.0).astype(BF16)
    parent_mask = iota((256, 128), 1) // 32 == iota((256, 128), 0) // 64
    for octet in range(7):
        for k in range(8):
            row = ef_ref[pl.ds(8 * octet + k, 1), :]
            high_ref[pl.ds(32 * k, 32), :] = jnp.where(spot, row, 0.0).astype(BF16)
        stack_ref[octet] = jnp.where(parent_mask, dot(high_ref[pl.ds(0, 256), :], unit), 0.0).astype(BF16)

    index_copy.wait()
    for k in range(2):
        shock_copy(k).wait_recv()
    for c in range(8):
        for kind in range(2):
            load(c, kind).wait()

        @pl.loop(4 * c, 4 * c + 4, unroll=2)
        def _(g):
            total = dot(shock_ref[32 + g], self_v[g])
            for j in range(3):
                total = total + dot(shock_ref[index_s[j, g]], near_v[g, j])
            near_ref[g] = total

    wait_all(upper_ref.at[pl.ds(0, 15)], out_recv)
    mask = iota((256, 128), 1) // 32 == 2
    node_ref[0] = jnp.zeros((16, 128), BF16)
    top_ref[0] = jnp.zeros((16, 1024), F32)
    coefs = jnp.where(mask, upper_ref[:, :, 128:256].reshape(256, 128).astype(F32), 0.0).astype(BF16)
    top_ref[16:32] = dot(coefs, spread_ref[0:128, :]).reshape(16, 16, 1024)
    for k in range(16):
        for j in range(4):
            node_ref[64 + 4 * k + j] = jnp.where(group == j, upper_ref[k, :, 0:128].astype(F32), 0.0).astype(BF16)
        for j in range(2):
            node_ref[32 + 2 * k + j] = jnp.where(group == j, upper_ref[k, :, 128:256].astype(F32), 0.0).astype(BF16)

    def parents(count):
        made = []
        for g in range(count, 2 * count):
            total = apply(top_ref[2 * g], uf_ref[pl.ds(2 * g - 8, 1), :])
            total = total + apply(top_ref[2 * g + 1], uf_ref[pl.ds(2 * g - 7, 1), :])
            made.append(fold(total))
        wide = spread(jnp.concatenate(made, axis=0), first_group(16 * count), matrix)
        top_ref[count : 2 * count] = wide.reshape(count, 16, 1024)

    parents(8)
    parents(4)

    rows = [node_ref[partner_ref[f, nodes[k] - 4]] for k in (4, 3) for f in range(8)]
    wide56_ref[...] = dot(jnp.concatenate(rows, axis=0), spread_ref[0:128, :]).reshape(16, 16, 1024)
    fields = []
    for k in range(5):
        load_upper(k).wait()
        blocks = couple_ref[k].astype(F32)
        total = None
        for f in range(8):
            if k == 4:
                wide = wide56_ref[f]
            elif k == 3:
                wide = wide56_ref[8 + f]
            else:
                wide = top_ref[partner_ref[f, nodes[k] - 4]]
            term = apply(wide, blocks[f : f + 1, :])
            total = term if total is None else total + term
        fields.append(fold(total))

    gather = gather_ref[...]

    def turn(field, row):
        return jnp.concatenate([field * row[:, t * 128 : t * 128 + 128] for t in range(8)], axis=1)

    def step(field, row):
        high, low = halves(turn(field, row))
        both = dot(jnp.concatenate([high, low], axis=0), gather)
        return both[0:16] + both[16:32]

    down = fields[0]
    for k in range(1, 5):
        down = fields[k] + step(down, uf_ref[pl.ds(nodes[k] - 8, 1), :])
    current = step(down, ef_ref[pl.ds(62, 1), :])

    for number in (4, 3, 2, 1, 0):
        near, far, tiles, base = CLASSES[number]
        count = 2 * (far - near + 1)
        wait_all(far_part(far_ref, number), far_recv.at[number])
        for t in range(tiles):
            total = sum_ref[t]
            for k in range(count):
                total = total + far_ref[base + k * tiles + t].astype(F32)
            sum_ref[t] = total

    half_mask = [iota((8, 128), 0) == 4 * a + iota((8, 128), 1) // 32 for a in range(2)]

    def source_row(p, j, a):
        if p < 32:
            return sum_ref[8 + 4 * (p // 16) + 2 * j + a, p % 16 : p % 16 + 1, :]
        if p < 48:
            return sum_ref[4 + 2 * j + a, p - 32 : p - 31, :]
        if p < 56:
            return sum_ref[2 + a, j * 8 + p - 48 : j * 8 + p - 47, :]
        row = (2 * j + a) * 4
        if p < 60:
            return sum_ref[1, row + p - 56 : row + p - 55, :]
        return sum_ref[0, row + p - 60 : row + p - 59, :]

    for p in range(63):
        for j in range(2):
            for a in range(2):
                inject_ref[pl.ds(16 * p + 8 * j, 8), 128 * a : 128 * a + 128] = jnp.where(
                    half_mask[a], source_row(p, j, a), 0.0
                )
    high, low = halves(inject_ref[...])
    local_ref[...] = dot(high, select_ref[...]) + dot(low, select_ref[...])

    current = current + local_ref[pl.ds(16 * 62, 16), :]
    for level in range(4, 2, -1):
        first, after = LEVEL_ROW[level], LEVEL_ROW[level + 1]
        for c in range(after - first):
            parent = current[16 * (c // 2) : 16 * (c // 2) + 16]
            high, low = halves(turn(parent, ef_ref[pl.ds(first + c, 1), :]))
            high_ref[pl.ds(16 * c, 16), :] = high
            low_ref[pl.ds(16 * c, 16), :] = low
        rows = 16 * (after - first)
        current = (
            local_ref[pl.ds(16 * first, rows), :]
            + dot(high_ref[pl.ds(0, rows), :], gather)
            + dot(low_ref[pl.ds(0, rows), :], gather)
        )

    def side_by_side(ref_rows):
        low_pair = jnp.where(group == 0, ref_rows[0:16], ref_rows[16:32])
        high_pair = jnp.where(group == 2, ref_rows[32:48], ref_rows[48:64])
        return jnp.where(group < 2, low_pair, high_pair)

    def children(field, octet):
        high, low = halves(field)
        both = lax.dot_general(
            jnp.concatenate([high, low], axis=0),
            stack_ref[octet],
            (((1,), (1,)), ((), ())),
            preferred_element_type=F32,
        )
        both = both[0:16] + both[16:32]
        return [
            both[:, 128 * half : 128 * half + 128]
            + side_by_side(local_ref[pl.ds(16 * (8 * octet + 4 * half), 64), :])
            for half in range(2)
        ]

    fields = children(side_by_side(current), 6)
    fields = [tile for j in range(2) for tile in children(fields[j], 4 + j)]
    fields = [tile for j in range(4) for tile in children(fields[j], j)]
    for quad in range(8):
        high, low = halves(jnp.concatenate([jnp.where(group == k, fields[quad], 0.0) for k in range(4)], axis=0))
        basis = v_ref[4 * quad : 4 * quad + 4].reshape(128, 256)
        done = dot(jnp.concatenate([high, low], axis=1), jnp.concatenate([basis, basis], axis=0))
        for k in range(4):
            lanes = pl.ds((4 * quad + k) * 256, 256)
            out_ref[:, lanes] = near_ref[4 * quad + k] + done[16 * k : 16 * k + 16]

    wait_all(lifts_ref.at[pl.ds(0, 7)], in_send)
    wait_all(upper_ref.at[pl.ds(0, 15)], out_send)
    for k in range(2):
        shock_copy(k).wait_send()
    for number in range(5):
        wait_all(far_part(send_ref, number), far_send.at[number])


def local(
    shocks,
    leaf_basis,
    self_block,
    near_block,
    near_offset,
    near_count,
    local_transfer,
    local_coupling,
    far_device,
    far_slot,
    upper_transfer,
    upper_coupling,
    upper_partner,
):
    return pl.pallas_call(
        kernel,
        out_shape=jax.ShapeDtypeStruct((16, 8192), F32),
        in_specs=[VMEM] * 9 + [SMEM] + [ANY] * 4,
        out_specs=VMEM,
        scratch_shapes=[
            pltpu.VMEM((64, 8, 1024), BF16),
            pltpu.VMEM((32, 256, 256), BF16),
            pltpu.VMEM((32, 3, 256, 256), BF16),
            pltpu.VMEM((5, 8, 1024), BF16),
            pltpu.VMEM((64, 1024), F32),
            pltpu.VMEM((120, 1024), F32),
            pltpu.VMEM((1024, 1024), F32),
            pltpu.VMEM((512, 512), F32),
            pltpu.VMEM((256, 1024), BF16),
            pltpu.VMEM((1024, 128), BF16),
            pltpu.VMEM((256, 128), BF16),
            pltpu.VMEM((TILES, 16, 128), BF16),
            pltpu.VMEM((TILES, 16, 128), BF16),
            pltpu.VMEM((16, 16, 128), F32),
            pltpu.VMEM((97, 16, 256), BF16),
            pltpu.VMEM((16, 128), F32),
            pltpu.VMEM((8, 16, 128), F32),
            pltpu.VMEM((16, 256), BF16),
            pltpu.VMEM((16, 16, 256), BF16),
            pltpu.VMEM((8, 128), jnp.int32),
            pltpu.SMEM((8, 128), jnp.int32),
            pltpu.VMEM((128, 16, 128), BF16),
            pltpu.VMEM((32, 16, 1024), F32),
            pltpu.VMEM((16, 16, 1024), F32),
            pltpu.VMEM((1008, 256), F32),
            pltpu.VMEM((1008, 128), F32),
            pltpu.VMEM((256, 1024), BF16),
            pltpu.VMEM((256, 1024), BF16),
            pltpu.VMEM((32, 16, 256), F32),
            pltpu.VMEM((7, 256, 128), BF16),
            pltpu.SemaphoreType.DMA((3, 8)),
            pltpu.SemaphoreType.DMA((5,)),
            pltpu.SemaphoreType.DMA,
            pltpu.SemaphoreType.DMA((5,)),
            pltpu.SemaphoreType.DMA((5,)),
            pltpu.SemaphoreType.DMA((2,)),
            pltpu.SemaphoreType.DMA((2,)),
            pltpu.SemaphoreType.DMA,
            pltpu.SemaphoreType.DMA,
            pltpu.SemaphoreType.DMA,
            pltpu.SemaphoreType.DMA,
        ],
        compiler_params=pltpu.CompilerParams(
            vmem_limit_bytes=56 * 2**20, collective_id=0, has_side_effects=True
        ),
        name="whole",
    )(
        shocks, leaf_basis, local_transfer, upper_transfer, far_device.T, far_slot.T, jnp.asarray(LANES),
        near_offset.T, near_count.reshape(1, 32), upper_partner.T, local_coupling, upper_coupling,
        self_block, near_block,
    )


def solution(mesh):
    both = ("outer", "inner")
    placed = (
        P(None, both),
        P(both, None, None),
        P(both, None, None),
        P(both, None, None, None),
        P(both, None),
        P(both),
        P(both, None),
        P(both, None, None),
        P(both, None),
        P(both, None),
        P(),
        P(),
        P(),
    )
    return jax.shard_map(
        local, mesh=mesh, in_specs=placed, out_specs=P(None, both), check_vma=False
    )
```

```python
import jax
import jax.numpy as jnp
import numpy as np
from jax import lax
from jax.experimental import pallas as pl
from jax.experimental.pallas import tpu as pltpu
from jax.sharding import PartitionSpec as P

F32 = jnp.float32
BF16 = jnp.bfloat16
MESH = pl.DeviceIdType.MESH
VMEM = pl.BlockSpec(memory_space=pltpu.VMEM)
SMEM = pl.BlockSpec(memory_space=pltpu.SMEM)
ANY = pl.BlockSpec(memory_space=pl.ANY)

CLASSES = ((1, 2, 16, 0), (3, 4, 8, 64), (5, 8, 4, 96), (9, 16, 2, 128), (17, 32, 1, 160))
TILES = 192


def slot_of(offset):
    for near, far, tiles, base in CLASSES:
        if near <= abs(offset) <= far:
            count = far - near + 1
            place = offset + far if offset < 0 else offset - near + count
            return base + place * tiles
    return None


LEVEL_ROW = (0, 32, 48, 56, 60, 62, 63)


def lane_table():
    table = np.zeros((8, 768), np.int32)
    for lane in range(768):
        if lane < 256:
            item, part, scale, shift = lane, 0, 32, 64
        elif lane < 384:
            item, part, scale, shift = lane, 0, 16, 64 - 32
        elif lane < 512:
            item, part = 384 + (lane - 384) % 64, (lane - 384) // 64
            scale, shift = 16, 128 + 8 * part - 48
        elif lane < 640:
            item, part = 448 + (lane - 512) % 32, (lane - 512) // 32
            scale, shift = 16, 256 + 4 * part - 56
        else:
            item, part = 480 + (lane - 640) % 32, (lane - 640) // 32
            scale, shift = 16, 512 + 4 * part - 60
        if item >= 504:
            scale, shift = 0, -1000000
        table[0, lane], table[1, lane], table[2, lane], table[3, lane] = item // 8, item % 8, scale, shift
    return table


LANES = lane_table()

def iota(shape, dim):
    return lax.broadcasted_iota(jnp.int32, shape, dim)


def halves(x):
    high = x.astype(BF16)
    low = (x - high.astype(F32)).astype(BF16)
    return high, low


def dot(a, b):
    return jnp.dot(a, b, preferred_element_type=F32)


def spread(coefs, mask, matrix):
    high, low = halves(jnp.where(mask, coefs, 0.0))
    return dot(jnp.concatenate([high, low], axis=1), matrix)


def fold(x):
    x = x + pltpu.roll(x, 64, 1)
    return x + pltpu.roll(x, 32, 1)


def apply(wide, row):
    total = wide[:, 0:128] * row[:, 0:128]
    for t in range(1, 8):
        total = total + wide[:, t * 128 : t * 128 + 128] * row[:, t * 128 : t * 128 + 128]
    return total


def first_group(rows):
    return iota((rows, 128), 1) < 32


def kernel(
    x_ref, v_ref, e_ref, ut_ref, fd_ref, fs_ref, lane_ref, off_ref, count_ref, partner_ref,
    b_hbm, uc_hbm, self_hbm, near_hbm,
    out_ref,
    b_ref, self_v, near_v, couple_ref, ef_ref, uf_ref, wide_ref, prod_ref, spread_ref, gather_ref, select_ref,
    send_ref, far_ref, sum_ref, shock_ref, lift_ref, lifts_ref, pack_ref, upper_ref,
    index_v, index_s, node_ref, top_ref, wide56_ref,
    inject_ref, local_ref, high_ref, low_ref, near_ref, stack_ref,
    load_sem, couple_sem, index_sem, far_send, far_recv, shock_send, shock_recv, in_send, in_recv,
    out_send, out_recv,
):
    outer = lax.axis_index("outer")
    inner = lax.axis_index("inner")
    me = outer * 8 + inner
    nodes = [lax.div(128 + me, 2 ** (7 - level)) for level in range(2, 7)]

    def place(index):
        return (lax.div(index, 8), lax.rem(index, 8))

    def load_basis():
        return pltpu.make_async_copy(b_hbm, b_ref.at[pl.ds(0, 63)], load_sem.at[2, 0])

    def load_upper(k):
        return pltpu.make_async_copy(uc_hbm.at[nodes[k] - 4], couple_ref.at[k], couple_sem.at[k])

    def load(c, kind):
        source, target = (self_hbm, self_v) if kind == 0 else (near_hbm, near_v)
        return pltpu.make_async_copy(
            source.at[pl.ds(4 * c, 4)], target.at[pl.ds(4 * c, 4)], load_sem.at[kind, c]
        )

    barrier = pltpu.get_barrier_semaphore()

    @pl.loop(1, 33)
    def _(step):
        pl.semaphore_signal(barrier, inc=1, device_id=place(lax.rem(me + step, 128)), device_id_type=MESH)
        pl.semaphore_signal(barrier, inc=1, device_id=place(lax.rem(me + 128 - step, 128)), device_id_type=MESH)

    @pl.loop(5, 12)
    def _(step):
        pl.semaphore_signal(barrier, inc=1, device_id=(lax.rem(outer + step, 16), inner), device_id_type=MESH)

    load_basis().start()
    for k in range(5):
        load_upper(k).start()
    for c in range(8):
        for kind in range(2):
            load(c, kind).start()

    unit = jnp.where(iota((32, 1024), 0) == iota((32, 1024), 1) // 32, 1.0, 0.0).astype(BF16)
    for k in range(8):
        spread_ref[32 * k : 32 * k + 32, :] = unit
    gather_ref[...] = jnp.where(iota((1024, 128), 0) // 32 == iota((1024, 128), 1) % 32, 1.0, 0.0).astype(BF16)
    unit = jnp.where(iota((32, 128), 0) == iota((32, 128), 1) % 32, 1.0, 0.0).astype(BF16)
    for k in range(8):
        select_ref[32 * k : 32 * k + 32, :] = unit

    near_row = iota((3, 32), 1) + off_ref[...] + 32
    source = me * 32 - 32 + near_row
    live = (iota((3, 32), 0) < count_ref[...]) & (source >= 0) & (source < 4096)
    index_v[...] = jnp.zeros((8, 128), jnp.int32)
    index_v[0:3, 0:32] = jnp.where(live, near_row, 96)
    index_copy = pltpu.make_async_copy(index_v, index_s, index_sem)
    index_copy.start()
    for g in range(32):
        shock_ref[32 + g] = x_ref[:, 256 * g : 256 * g + 256]
    shock_ref[96] = jnp.zeros((16, 256), BF16)
    ef_ref[pl.ds(0, 63), :] = e_ref[...].astype(F32)
    uf_ref[...] = ut_ref[...].astype(F32)
    matrix = spread_ref[...]

    group_mask = iota((64, 128), 1) // 32 == iota((64, 128), 0) // 16
    for group in range(8):
        block = shock_ref[32 + 4 * group : 36 + 4 * group].reshape(64, 256)
        basis = v_ref[4 * group : 4 * group + 4].reshape(128, 256)
        coefs = lax.dot_general(block, basis, (((1,), (1,)), ((), ())), preferred_element_type=F32)
        wide_ref[pl.ds(64 * group, 64), :] = spread(coefs, group_mask, matrix)

    for level in range(5):
        first, after = LEVEL_ROW[level], LEVEL_ROW[level + 1]
        parents = []
        for g in range((after - first) // 2):
            total = None
            for child in (first + 2 * g, first + 2 * g + 1):
                term = apply(wide_ref[pl.ds(16 * child, 16), :], ef_ref[pl.ds(child, 1), :])
                total = term if total is None else total + term
            parents.append(fold(total))
        rows = 16 * len(parents)
        coefs = jnp.concatenate(parents, axis=0) if len(parents) > 1 else parents[0]
        wide_ref[pl.ds(16 * after, rows), :] = spread(coefs, first_group(rows), matrix)
    lift_ref[...] = fold(apply(wide_ref[pl.ds(16 * 62, 16), :], ef_ref[pl.ds(62, 1), :]))

    def lift_copy(k):
        return pltpu.make_async_remote_copy(
            src_ref=lift_ref,
            dst_ref=lifts_ref.at[inner],
            send_sem=in_send,
            recv_sem=in_recv,
            device_id=(outer, lax.rem(inner + k, 8)),
            device_id_type=MESH,
        )

    def pack_copy(k):
        return pltpu.make_async_remote_copy(
            src_ref=pack_ref,
            dst_ref=upper_ref.at[outer],
            send_sem=out_send,
            recv_sem=out_recv,
            device_id=(lax.rem(outer + k, 16), inner),
            device_id_type=MESH,
        )

    def shock_copy(k):
        return pltpu.make_async_remote_copy(
            src_ref=shock_ref.at[pl.ds(32, 32)],
            dst_ref=shock_ref.at[pl.ds(64 * k, 32)],
            send_sem=shock_send.at[k],
            recv_sem=shock_recv.at[k],
            device_id=place(lax.rem(me + (1 if k == 0 else 127), 128)),
            device_id_type=MESH,
        )

    def far_start(number):
        near, far, tiles, base = CLASSES[number]
        count = far - near + 1

        @pl.loop(0, 2 * count)
        def _(index):
            offset = jnp.where(index < count, index - far, index - count + near)
            span = pl.ds(base + index * tiles, tiles)
            pltpu.make_async_remote_copy(
                src_ref=send_ref.at[span],
                dst_ref=far_ref.at[span],
                send_sem=far_send.at[number],
                recv_sem=far_recv.at[number],
                device_id=place(lax.rem(me + offset + 128, 128)),
                device_id_type=MESH,
            ).start()

    def wait_all(ref, sem):
        pltpu.make_async_copy(ref, ref, sem).wait()

    def far_part(ref, number):
        near, far, tiles, base = CLASSES[number]
        return ref.at[pl.ds(base, 2 * (far - near + 1) * tiles)]

    pl.semaphore_wait(barrier, 71)
    for k in range(1, 8):
        lift_copy(k).start()
    for k in range(2):
        shock_copy(k).start()
    lifts_ref[inner] = lift_ref[...]

    table = lane_ref[...]
    pick = (iota((8, 768), 0) == table[1:2, :]).astype(F32)
    mine = (iota((63, 768), 0) == table[0:1, :]).astype(F32)
    offset = jnp.sum(dot((fd_ref[...] - me + 32).astype(F32), mine) * pick, axis=0, keepdims=True)
    slot = jnp.sum(dot(fs_ref[...].astype(F32), mine) * pick, axis=0, keepdims=True)
    target = table[2:3, :] * (offset.astype(jnp.int32) - 32) + slot.astype(jnp.int32) + table[3:4, :]

    low_half = iota((8, 128), 1) < 64
    even = (iota((8, 128), 1) // 32) % 2 == 0

    def couple(start, stop):
        @pl.loop(start, stop, unroll=8)
        def _(p):
            blocks = b_ref[p].astype(F32)
            for quad in range(4):
                sums = [apply(blocks, wide_ref[pl.ds(p * 16 + 4 * quad + k, 1), :]) for k in range(4)]
                a0, a1, a2, a3 = sums[2], sums[1], sums[0], sums[3]
                w02 = jnp.where(low_half, a0, a2) + pltpu.roll(jnp.where(low_half, a2, a0), 64, 1)
                w13 = jnp.where(low_half, a1, a3) + pltpu.roll(jnp.where(low_half, a3, a1), 64, 1)
                w20 = pltpu.roll(w02, 64, 1)
                done = jnp.where(even, w20, w13) + pltpu.roll(jnp.where(even, w13, w02), 32, 1)
                prod_ref[pl.ds(p * 8, 8), pl.ds(128 * quad, 128)] = done

    def chosen(rows, start, lanes, high, low):
        hot = jnp.where(iota((rows, lanes), 0) == target[:, start : start + lanes], 1.0, 0.0)
        hot = hot.astype(BF16)
        return dot(hot, high) + dot(hot, low)

    def put(offset, tile, value):
        if offset == 0:
            sum_ref[tile] = value
        else:
            send_ref[slot_of(offset) + tile] = value.astype(BF16)

    wide_ref[1008:1024, :] = jnp.zeros((16, 1024), F32)
    load_basis().wait()
    b_ref[63] = jnp.zeros((8, 1024), BF16)
    couple(32, 64)
    wait_all(lifts_ref.at[pl.ds(0, 7)], in_recv)
    sixth = [lifts_ref[2 * j] + lifts_ref[2 * j + 1] for j in range(4)]
    wide = spread(jnp.concatenate(sixth, axis=0), first_group(64), matrix)

    def link(first, k):
        return uf_ref[pl.ds(first + k, 1), :]

    fifth = [
        fold(
            apply(wide[32 * j : 32 * j + 16], link(56 + 4 * outer, 2 * j))
            + apply(wide[32 * j + 16 : 32 * j + 32], link(56 + 4 * outer, 2 * j + 1))
        )
        for j in range(2)
    ]
    wide = spread(jnp.concatenate(fifth, axis=0), first_group(32), matrix)
    fourth = fold(apply(wide[0:16], link(24 + 2 * outer, 0)) + apply(wide[16:32], link(24 + 2 * outer, 1)))
    group = iota((16, 128), 1) // 32
    pack_ref[:, 0:128] = jnp.where(
        group < 2, jnp.where(group == 0, sixth[0], sixth[1]), jnp.where(group == 2, sixth[2], sixth[3])
    ).astype(BF16)
    pack_ref[:, 128:256] = jnp.where(
        group < 2, jnp.where(group == 0, fifth[0], fifth[1]), jnp.where(group == 2, fourth, 0.0)
    ).astype(BF16)
    for k in range(1, 16):
        pack_copy(k).start()
    upper_ref[outer] = pack_ref[...]

    part = jnp.concatenate([prod_ref[480:512, j * 128 : j * 128 + 128] for j in range(4)], axis=0)
    out = chosen(1040, 640, 128, *halves(part))
    for k in range(65):
        put(k - 32, 0, out[k * 16 : k * 16 + 16, :])
    part = jnp.concatenate([prod_ref[448:480, j * 128 : j * 128 + 128] for j in range(4)], axis=0)
    out = chosen(528, 512, 128, *halves(part))
    for k in range(33):
        put(k - 16, 1, out[k * 16 : k * 16 + 16, :])
    part = jnp.concatenate([prod_ref[384:448, j * 256 : j * 256 + 256] for j in range(2)], axis=0)
    out = chosen(272, 384, 128, *halves(part))
    for k in range(17):
        for j in range(2):
            put(k - 8, 2 + j, out[k * 16 : k * 16 + 16, j * 128 : j * 128 + 128])
    out = chosen(144, 256, 128, *halves(prod_ref[256:384, :]))
    for k in range(9):
        for j in range(4):
            put(k - 4, 4 + j, out[k * 16 : k * 16 + 16, j * 128 : j * 128 + 128])
    for number in (1, 2, 3, 4):
        far_start(number)

    couple(0, 32)
    out = chosen(160, 0, 256, *halves(prod_ref[0:256, :]))
    for k in range(5):
        for half in range(2):
            for j in range(4):
                row = k * 32 + half * 16
                put(k - 2, 8 + 4 * half + j, out[row : row + 16, j * 128 : j * 128 + 128])
    far_start(0)

    index_copy.wait()
    for k in range(2):
        shock_copy(k).wait_recv()
    for c in range(8):
        for kind in range(2):
            load(c, kind).wait()

        @pl.loop(4 * c, 4 * c + 4, unroll=2)
        def _(g):
            total = dot(shock_ref[32 + g], self_v[g])
            for j in range(3):
                total = total + dot(shock_ref[index_s[j, g]], near_v[g, j])
            near_ref[g] = total

    spot = iota((32, 1024), 1) // 32 == iota((32, 1024), 0)
    unit = jnp.where(iota((1024, 128), 0) % 32 == iota((1024, 128), 1) % 32, 1.0, 0.0).astype(BF16)
    parent_mask = iota((256, 128), 1) // 32 == iota((256, 128), 0) // 64
    for octet in range(7):
        for k in range(8):
            row = ef_ref[pl.ds(8 * octet + k, 1), :]
            high_ref[pl.ds(32 * k, 32), :] = jnp.where(spot, row, 0.0).astype(BF16)
        stack_ref[octet] = jnp.where(parent_mask, dot(high_ref[pl.ds(0, 256), :], unit), 0.0).astype(BF16)

    wait_all(upper_ref.at[pl.ds(0, 15)], out_recv)
    mask = iota((256, 128), 1) // 32 == 2
    node_ref[0] = jnp.zeros((16, 128), BF16)
    top_ref[0] = jnp.zeros((16, 1024), F32)
    coefs = jnp.where(mask, upper_ref[:, :, 128:256].reshape(256, 128).astype(F32), 0.0).astype(BF16)
    top_ref[16:32] = dot(coefs, spread_ref[0:128, :]).reshape(16, 16, 1024)
    for k in range(16):
        for j in range(4):
            node_ref[64 + 4 * k + j] = jnp.where(group == j, upper_ref[k, :, 0:128].astype(F32), 0.0).astype(BF16)
        for j in range(2):
            node_ref[32 + 2 * k + j] = jnp.where(group == j, upper_ref[k, :, 128:256].astype(F32), 0.0).astype(BF16)

    def parents(count):
        made = []
        for g in range(count, 2 * count):
            total = apply(top_ref[2 * g], uf_ref[pl.ds(2 * g - 8, 1), :])
            total = total + apply(top_ref[2 * g + 1], uf_ref[pl.ds(2 * g - 7, 1), :])
            made.append(fold(total))
        wide = spread(jnp.concatenate(made, axis=0), first_group(16 * count), matrix)
        top_ref[count : 2 * count] = wide.reshape(count, 16, 1024)

    parents(8)
    parents(4)

    rows = [node_ref[partner_ref[f, nodes[k] - 4]] for k in (4, 3) for f in range(8)]
    wide56_ref[...] = dot(jnp.concatenate(rows, axis=0), spread_ref[0:128, :]).reshape(16, 16, 1024)
    fields = []
    for k in range(5):
        load_upper(k).wait()
        blocks = couple_ref[k].astype(F32)
        total = None
        for f in range(8):
            if k == 4:
                wide = wide56_ref[f]
            elif k == 3:
                wide = wide56_ref[8 + f]
            else:
                wide = top_ref[partner_ref[f, nodes[k] - 4]]
            term = apply(wide, blocks[f : f + 1, :])
            total = term if total is None else total + term
        fields.append(fold(total))

    gather = gather_ref[...]

    def turn(field, row):
        return jnp.concatenate([field * row[:, t * 128 : t * 128 + 128] for t in range(8)], axis=1)

    def step(field, row):
        high, low = halves(turn(field, row))
        both = dot(jnp.concatenate([high, low], axis=0), gather)
        return both[0:16] + both[16:32]

    down = fields[0]
    for k in range(1, 5):
        down = fields[k] + step(down, uf_ref[pl.ds(nodes[k] - 8, 1), :])
    current = step(down, ef_ref[pl.ds(62, 1), :])

    for number in (4, 3, 2, 1, 0):
        near, far, tiles, base = CLASSES[number]
        count = 2 * (far - near + 1)
        wait_all(far_part(far_ref, number), far_recv.at[number])
        for t in range(tiles):
            total = sum_ref[t]
            for k in range(count):
                total = total + far_ref[base + k * tiles + t].astype(F32)
            sum_ref[t] = total

    half_mask = [iota((8, 128), 0) == 4 * a + iota((8, 128), 1) // 32 for a in range(2)]

    def source_row(p, j, a):
        if p < 32:
            return sum_ref[8 + 4 * (p // 16) + 2 * j + a, p % 16 : p % 16 + 1, :]
        if p < 48:
            return sum_ref[4 + 2 * j + a, p - 32 : p - 31, :]
        if p < 56:
            return sum_ref[2 + a, j * 8 + p - 48 : j * 8 + p - 47, :]
        row = (2 * j + a) * 4
        if p < 60:
            return sum_ref[1, row + p - 56 : row + p - 55, :]
        return sum_ref[0, row + p - 60 : row + p - 59, :]

    for p in range(63):
        for j in range(2):
            for a in range(2):
                inject_ref[pl.ds(16 * p + 8 * j, 8), 128 * a : 128 * a + 128] = jnp.where(
                    half_mask[a], source_row(p, j, a), 0.0
                )
    high, low = halves(inject_ref[...])
    local_ref[...] = dot(high, select_ref[...]) + dot(low, select_ref[...])

    current = current + local_ref[pl.ds(16 * 62, 16), :]
    for level in range(4, 2, -1):
        first, after = LEVEL_ROW[level], LEVEL_ROW[level + 1]
        for c in range(after - first):
            parent = current[16 * (c // 2) : 16 * (c // 2) + 16]
            high, low = halves(turn(parent, ef_ref[pl.ds(first + c, 1), :]))
            high_ref[pl.ds(16 * c, 16), :] = high
            low_ref[pl.ds(16 * c, 16), :] = low
        rows = 16 * (after - first)
        current = (
            local_ref[pl.ds(16 * first, rows), :]
            + dot(high_ref[pl.ds(0, rows), :], gather)
            + dot(low_ref[pl.ds(0, rows), :], gather)
        )

    def side_by_side(ref_rows):
        low_pair = jnp.where(group == 0, ref_rows[0:16], ref_rows[16:32])
        high_pair = jnp.where(group == 2, ref_rows[32:48], ref_rows[48:64])
        return jnp.where(group < 2, low_pair, high_pair)

    def children(field, octet):
        high, low = halves(field)
        both = lax.dot_general(
            jnp.concatenate([high, low], axis=0),
            stack_ref[octet],
            (((1,), (1,)), ((), ())),
            preferred_element_type=F32,
        )
        both = both[0:16] + both[16:32]
        return [
            both[:, 128 * half : 128 * half + 128]
            + side_by_side(local_ref[pl.ds(16 * (8 * octet + 4 * half), 64), :])
            for half in range(2)
        ]

    fields = children(side_by_side(current), 6)
    fields = [tile for j in range(2) for tile in children(fields[j], 4 + j)]
    fields = [tile for j in range(4) for tile in children(fields[j], j)]
    for quad in range(8):
        high, low = halves(jnp.concatenate([jnp.where(group == k, fields[quad], 0.0) for k in range(4)], axis=0))
        basis = v_ref[4 * quad : 4 * quad + 4].reshape(128, 256)
        done = dot(jnp.concatenate([high, low], axis=1), jnp.concatenate([basis, basis], axis=0))
        for k in range(4):
            lanes = pl.ds((4 * quad + k) * 256, 256)
            out_ref[:, lanes] = near_ref[4 * quad + k] + done[16 * k : 16 * k + 16]

    wait_all(lifts_ref.at[pl.ds(0, 7)], in_send)
    wait_all(upper_ref.at[pl.ds(0, 15)], out_send)
    for k in range(2):
        shock_copy(k).wait_send()
    for number in range(5):
        wait_all(far_part(send_ref, number), far_send.at[number])


def local(
    shocks,
    leaf_basis,
    self_block,
    near_block,
    near_offset,
    near_count,
    local_transfer,
    local_coupling,
    far_device,
    far_slot,
    upper_transfer,
    upper_coupling,
    upper_partner,
):
    return pl.pallas_call(
        kernel,
        out_shape=jax.ShapeDtypeStruct((16, 8192), F32),
        in_specs=[VMEM] * 9 + [SMEM] + [ANY] * 4,
        out_specs=VMEM,
        scratch_shapes=[
            pltpu.VMEM((64, 8, 1024), BF16),
            pltpu.VMEM((32, 256, 256), BF16),
            pltpu.VMEM((32, 3, 256, 256), BF16),
            pltpu.VMEM((5, 8, 1024), BF16),
            pltpu.VMEM((64, 1024), F32),
            pltpu.VMEM((120, 1024), F32),
            pltpu.VMEM((1024, 1024), F32),
            pltpu.VMEM((512, 512), F32),
            pltpu.VMEM((256, 1024), BF16),
            pltpu.VMEM((1024, 128), BF16),
            pltpu.VMEM((256, 128), BF16),
            pltpu.VMEM((TILES, 16, 128), BF16),
            pltpu.VMEM((TILES, 16, 128), BF16),
            pltpu.VMEM((16, 16, 128), F32),
            pltpu.VMEM((97, 16, 256), BF16),
            pltpu.VMEM((16, 128), F32),
            pltpu.VMEM((8, 16, 128), F32),
            pltpu.VMEM((16, 256), BF16),
            pltpu.VMEM((16, 16, 256), BF16),
            pltpu.VMEM((8, 128), jnp.int32),
            pltpu.SMEM((8, 128), jnp.int32),
            pltpu.VMEM((128, 16, 128), BF16),
            pltpu.VMEM((32, 16, 1024), F32),
            pltpu.VMEM((16, 16, 1024), F32),
            pltpu.VMEM((1008, 256), F32),
            pltpu.VMEM((1008, 128), F32),
            pltpu.VMEM((256, 1024), BF16),
            pltpu.VMEM((256, 1024), BF16),
            pltpu.VMEM((32, 16, 256), F32),
            pltpu.VMEM((7, 256, 128), BF16),
            pltpu.SemaphoreType.DMA((3, 8)),
            pltpu.SemaphoreType.DMA((5,)),
            pltpu.SemaphoreType.DMA,
            pltpu.SemaphoreType.DMA((5,)),
            pltpu.SemaphoreType.DMA((5,)),
            pltpu.SemaphoreType.DMA((2,)),
            pltpu.SemaphoreType.DMA((2,)),
            pltpu.SemaphoreType.DMA,
            pltpu.SemaphoreType.DMA,
            pltpu.SemaphoreType.DMA,
            pltpu.SemaphoreType.DMA,
        ],
        compiler_params=pltpu.CompilerParams(
            vmem_limit_bytes=56 * 2**20, collective_id=0, has_side_effects=True
        ),
        name="whole",
    )(
        shocks, leaf_basis, local_transfer, upper_transfer, far_device.T, far_slot.T, jnp.asarray(LANES),
        near_offset.T, near_count.reshape(1, 32), upper_partner.T, local_coupling, upper_coupling,
        self_block, near_block,
    )


def solution(mesh):
    both = ("outer", "inner")
    placed = (
        P(None, both),
        P(both, None, None),
        P(both, None, None),
        P(both, None, None, None),
        P(both, None),
        P(both),
        P(both, None),
        P(both, None, None),
        P(both, None),
        P(both, None),
        P(),
        P(),
        P(),
    )
    return jax.shard_map(
        local, mesh=mesh, in_specs=placed, out_specs=P(None, both), check_vma=False
    )
```
